32 devices in a mesh: dp: 2 (over x), expert: 8 (over z, y), tensor: 2 (over core).
Axes of the slice: x: 2, y: 2, z: 4, core: 2. Of those that a mesh axis runs over, the one named last changes fastest.
Arguments:
- tokens: bfloat16 [2048, 2048], P(('dp', 'expert'), 'tensor'), may hold values from -6 to 6
- routes: int32 [2048, 4], P(('dp', 'expert')), may hold values from 0 to 7, all different within a row; in each aligned block of 128 rows (0 to 127, 128 to 255, ...) at most 80 rows name the same one
- gates: float32 [2048, 4], P(('dp', 'expert')), may hold values from 0.05 to 1
- w_in: bfloat16 [8, 768, 2048], P('expert', 'tensor'), may hold values from -0.125 to 0.125
- w_out: bfloat16 [8, 768, 2048], P('expert', 'tensor'), may hold values from -0.21875 to 0.21875
- cotangent: bfloat16 [2048, 2048], P(('dp', 'expert'), 'tensor'), may hold values from -1.796875 to 1.796875
Outputs:
- mixed: bfloat16 [2048, 2048], P(('dp', 'expert'), 'tensor')
- grad_tokens: bfloat16 [2048, 2048], P(('dp', 'expert'), 'tensor')
- grad_gates: float32 [2048, 4], P(('dp', 'expert'))
- grad_in: float32 [8, 768, 2048], P('expert', 'tensor', 'dp')
- grad_out: float32 [8, 768, 2048], P('expert', 'tensor', 'dp')
The draws below stay inside these ranges and needn't reach their ends.
Inputs may be any that keep to these rules, and one draw needn't show every extreme that they name: `routes`: each row names 4 different experts. The rows of one device (aligned blocks of 128 rows) name no expert more than 80 times, and in every draw some block names some expert exactly 80 times.
All inputs are finite; a program needn't handle non-finite values.
Results may differ from the reference program's by a relative error of at most 0.018.
Values may be sent and summed in bfloat16 or wider, within the bound.
No kernel may reach another device: no remote copies, remote signals or barrier semaphores. Data moves between devices by JAX's collectives and lax.ppermute only.
A program may use at most 64 MiB of HBM per device.

```python
import math
import jax
import jax.numpy as jnp
import numpy as np
from jax import lax

D = 2048
F = 768
TOPK = 4
TOK_DEV = 128
EXPERTS = 8
TOKENS = 2048
CAP = 80
N_DP = 2
N_EXPERT = 8


def strengthened(result, stream_key, source, target, shards_of, factor):
    owner, partner = [(jnp.arange(result.shape[axis_at]) // (result.shape[axis_at] // shards_of)).reshape([-1 if axis == axis_at else 1 for axis in range(result.ndim)]) for axis_at in (source, target)]
    chosen = jax.random.permutation(stream_key, shards_of)[partner]
    strong = (owner == chosen) | (owner == (partner + shards_of // 2) % shards_of)
    return jnp.where(strong, factor * result, result)


def block_scale(stream_key, shape, pieces, low, largest):
    def one(position, shards_of):
        draws = jax.random.uniform(jax.random.fold_in(jax.random.fold_in(stream_key, 6), position), (shards_of,), jnp.float32, low / len(pieces), largest / len(pieces))
        return jnp.repeat(jnp.exp(draws), shape[position] // shards_of).reshape((-1,) + (1,) * (len(shape) - position - 1))

    gain = one(*pieces[0])
    for cut in pieces[1:]:
        gain = gain * one(*cut)
    return gain


def shared_out(rng, own, number, rows, number_of, top, bound, skew):
    ranking = jax.random.permutation(rng, number_of)
    packed, common = portions_of(number_of, rows * top, bound, skew, True), portions_of(number_of, rows * top, bound, skew, False)
    places = jnp.arange(number_of)

    def named(tallies, turn):
        used = int((tallies > 0).sum())
        fixed = max(1, used // 4)
        passed = fixed + (places - fixed + turn * (used - fixed)) % max(1, number_of - fixed)
        return jnp.zeros((number_of,), jnp.int32).at[ranking[jnp.where(places < fixed, places, passed)]].set(jnp.asarray(tallies, jnp.int32))

    tallies = jnp.where(number % 4 == 0, named(packed, number // 4), named(common, number - number // 4 - 1))
    mixed = jax.random.permutation(jax.random.fold_in(own, 3), number_of)
    donor, sink = mixed[0:number_of // 2 * 2:2], mixed[1:number_of // 2 * 2:2]
    slack = jnp.minimum(tallies[donor] - 1, bound - tallies[sink]) // 2
    slack = jnp.where((donor == ranking[0]) | (sink == ranking[0]) | (tallies[sink] == 0), 0, jnp.maximum(slack, 0))
    passed = jax.random.randint(jax.random.fold_in(own, 4), (number_of // 2,), 0, 1 << 20) % (slack + 1)
    tallies = tallies.at[donor].add(-passed).at[sink].add(passed)
    items = jnp.searchsorted(jnp.cumsum(tallies), jnp.arange(rows * top), side="right").astype(jnp.int32)
    grid = items.reshape(top, rows).T
    grid = grid[jax.random.permutation(jax.random.fold_in(own, 1), rows)]
    turn = jax.random.randint(jax.random.fold_in(own, 2), (rows, 1), 0, top)
    return jnp.take_along_axis(grid, (jnp.arange(top)[None, :] + turn) % top, axis=1)


def portions_of(number_of, total, limit, slope, full):
    weights = [(1 << 20) // math.isqrt(standing ** slope) + 1 for standing in range(1, number_of + 1)]
    largest = limit if full else min(limit, max(-(-total // number_of), total * weights[0] // sum(weights)))
    least = 1 if total - largest >= number_of - 1 else 0
    given, surplus = [largest] + [least] * (number_of - 1), total - largest - least * (number_of - 1)
    while surplus > 0:
        movable = [i for i in range(1, number_of) if given[i] < largest] or [i for i in range(1, number_of) if given[i] < limit]
        mass, left = sum([weights[i] for i in movable]), surplus
        for i in movable:
            extra = min(limit - given[i], max(1, left * weights[i] // mass), surplus)
            given[i] = given[i] + extra
            surplus = surplus - extra
    return np.array(given)


def normal_values(stream_key, shape, width, reach, cuts=(), kind=jnp.bfloat16):
    result = width * jax.random.normal(stream_key, shape, jnp.float32)
    if cuts:
        result = result * block_scale(stream_key, shape, cuts, -0.22, 0.18)
    return jnp.clip(result, -reach, reach).astype(kind)


def noise_with(rng, shape, deviation, most, pieces, heavy, kind=jnp.bfloat16):
    entries = deviation * jax.random.normal(rng, shape, jnp.float32)
    if pieces:
        entries = entries * block_scale(rng, shape, pieces, -0.22, 0.18)
    return jnp.clip(strengthened(entries, jax.random.fold_in(rng, 3), *heavy), -most, most).astype(kind)


def setup_inputs(seed: int = 0) -> dict:
    key_list = jax.random.split(jax.random.key(seed), 7)
    tokens = noise_with(key_list[0], (TOKENS, D), 1.0, 6.0, ((0, 16), (1, 2)), (0, 1, 16, 2.0))
    routes_keys = jax.random.split(jax.random.fold_in(key_list[1], 1), TOKENS // TOK_DEV)
    routes_turns = jax.random.permutation(jax.random.fold_in(key_list[1], 3), TOKENS // TOK_DEV)
    routes = jax.vmap(lambda own, number: shared_out(jax.random.fold_in(key_list[1], 2), own, number, TOK_DEV, EXPERTS, TOPK, CAP, 2))(routes_keys, routes_turns).reshape((TOKENS, TOPK))
    gates = jnp.clip(jnp.exp(math.log(1.0) - 2.9957323 * jax.random.uniform(key_list[2], (TOKENS, TOPK), jnp.float32) ** block_scale(key_list[2], (TOKENS, TOPK), ((0, 16),), -0.2, 0.2)), 0.05, 1.0)
    w_in = normal_values(key_list[3], (EXPERTS, F, D), D ** -0.5, 0.125, ((0, 8), (1, 2)))
    w_out = normal_values(key_list[4], (EXPERTS, F, D), F ** -0.5, 0.21875, ((0, 8), (1, 2)))
    cotangent = noise_with(key_list[5], (TOKENS, D), 0.3, 1.796875, ((0, 16), (1, 2)), (0, 1, 16, 2.0))
    return {"tokens": tokens, "routes": routes, "gates": gates, "w_in": w_in, "w_out": w_out, "cotangent": cotangent}


def silu_slope(pre_value):
    logistic = jax.nn.sigmoid(pre_value)
    return logistic * (1.0 + pre_value * (1.0 - logistic))


def take_rows(table, index):
    return jax.vmap(lambda rows_table, row_index: rows_table[row_index])(table, index)


def reference(tokens, routes, gates, w_in, w_out, cotangent):
    blocks = N_DP * N_EXPERT
    pair_count = TOK_DEV * TOPK
    block_routes = routes.reshape(blocks, pair_count)
    one_hot = (block_routes[:, :, None] == jnp.arange(EXPERTS, dtype=jnp.int32)[None, None, :]).astype(jnp.int32)
    rank_before = jnp.cumsum(one_hot, axis=1) - one_hot
    slot_index = jnp.sum(rank_before * one_hot, axis=2).astype(jnp.int32)
    destination = (block_routes * CAP + slot_index).astype(jnp.int32)
    block_ids = jnp.broadcast_to(jnp.arange(blocks, dtype=jnp.int32)[:, None], (blocks, pair_count))
    pair_ids = jnp.broadcast_to(jnp.arange(pair_count, dtype=jnp.int32)[None, :], (blocks, pair_count))
    source = jnp.full((blocks, EXPERTS * CAP), pair_count, jnp.int32).at[block_ids, destination].set(pair_ids)
    source = source.reshape(blocks, EXPERTS, CAP).transpose(1, 0, 2)
    zero_rows = jnp.zeros((blocks, 1, D), tokens.dtype)
    tokens_pad = jnp.concatenate([tokens.reshape(blocks, TOK_DEV, D), zero_rows], axis=1)
    cotangent_pad = jnp.concatenate([cotangent.reshape(blocks, TOK_DEV, D), zero_rows], axis=1)
    gates_pad = jnp.concatenate([gates.reshape(blocks, pair_count), jnp.zeros((blocks, 1), jnp.float32)], axis=1)
    cotangent_wide = cotangent.reshape(blocks, TOK_DEV, D).astype(jnp.float32)
    slot_tok = slot_index.reshape(blocks, TOK_DEV, TOPK)
    gates_tok = gates.reshape(blocks, TOK_DEV, TOPK)

    def expert_step(carry, inputs):
        mixed_acc, tok_acc, gate_acc = carry
        expert_id, source_e, w_in_e, w_out_e = inputs
        source_row = (source_e // TOPK).astype(jnp.int32)
        rows = take_rows(tokens_pad, source_row).reshape(blocks * CAP, D)
        pre_value = jnp.dot(rows, w_in_e.T, preferred_element_type=jnp.float32)
        hidden = jax.nn.silu(pre_value).astype(jnp.bfloat16)
        expert_out = jnp.dot(hidden, w_out_e, preferred_element_type=jnp.float32).astype(jnp.bfloat16)
        gate_slots = take_rows(gates_pad, source_e).reshape(blocks * CAP, 1)
        cot_rows = take_rows(cotangent_pad, source_row).reshape(blocks * CAP, D)
        scaled = (gate_slots * cot_rows.astype(jnp.float32)).astype(jnp.bfloat16)
        grad_hidden = jnp.dot(scaled, w_out_e.T, preferred_element_type=jnp.float32)
        grad_pre = (grad_hidden * silu_slope(pre_value)).astype(jnp.bfloat16)
        grad_rows = jnp.dot(grad_pre, w_in_e, preferred_element_type=jnp.float32).astype(jnp.bfloat16)
        group_rows = rows.reshape(N_DP, N_EXPERT * CAP, D).astype(jnp.float32)
        group_pre = grad_pre.reshape(N_DP, N_EXPERT * CAP, F).astype(jnp.float32)
        group_hidden = hidden.reshape(N_DP, N_EXPERT * CAP, F).astype(jnp.float32)
        group_scaled = scaled.reshape(N_DP, N_EXPERT * CAP, D).astype(jnp.float32)
        in_part = jnp.einsum("grf,grd->gfd", group_pre, group_rows).astype(jnp.bfloat16)
        grad_in_e = jnp.sum(in_part.astype(jnp.float32), axis=0)
        out_part = jnp.einsum("grf,grd->gfd", group_hidden, group_scaled).astype(jnp.bfloat16)
        grad_out_e = jnp.sum(out_part.astype(jnp.float32), axis=0)
        hits = (block_routes == expert_id).reshape(blocks, TOK_DEV, TOPK)
        hit_wide = hits.astype(jnp.float32)
        tok_slot = jnp.sum(slot_tok * hits.astype(jnp.int32), axis=2).astype(jnp.int32)
        tok_gate = jnp.sum(gates_tok * hit_wide, axis=2)
        tok_mask = jnp.sum(hit_wide, axis=2)
        out_tok = take_rows(expert_out.reshape(blocks, CAP, D), tok_slot).astype(jnp.float32)
        mixed_acc = mixed_acc + tok_gate[:, :, None] * out_tok
        inner = jnp.sum(cotangent_wide * out_tok, axis=2)
        gate_acc = gate_acc + inner[:, :, None] * hit_wide
        back_tok = take_rows(grad_rows.reshape(blocks, CAP, D), tok_slot).astype(jnp.float32)
        tok_acc = tok_acc + tok_mask[:, :, None] * back_tok
        return (mixed_acc, tok_acc, gate_acc), (grad_in_e, grad_out_e)

    start_carry = (jnp.zeros((blocks, TOK_DEV, D), jnp.float32), jnp.zeros((blocks, TOK_DEV, D), jnp.float32), jnp.zeros((blocks, TOK_DEV, TOPK), jnp.float32))
    inputs = (jnp.arange(EXPERTS, dtype=jnp.int32), source, w_in, w_out)
    (mixed_acc, tok_acc, gate_acc), (grad_in, grad_out) = lax.scan(expert_step, start_carry, inputs)
    mixed = mixed_acc.reshape(TOKENS, D).astype(jnp.bfloat16)
    grad_tokens = tok_acc.reshape(TOKENS, D).astype(jnp.bfloat16)
    grad_gates = gate_acc.reshape(TOKENS, TOPK)
    return (mixed, grad_tokens, grad_gates, grad_in, grad_out)
```

```python
import jax
import jax.numpy as jnp
from jax import lax
from jax.sharding import PartitionSpec as P

BF16 = jnp.bfloat16
F32 = jnp.float32


def ring_order(count):
    if count % 2:
        return list(range(count))
    return list(range(0, count, 2)) + list(range(count - 1, 0, -2))


def swap_cores(value):
    return lax.ppermute(value, "tensor", [(0, 1), (1, 0)])


def rows_by_units(rows, weights):
    return lax.dot_general(rows, weights, (((1,), (1,)), ((), ())), preferred_element_type=F32)


def rows_by_width(rows, weights):
    return lax.dot_general(rows, weights, (((1,), (0,)), ((), ())), preferred_element_type=F32)


def over_rows(left, right):
    return lax.dot_general(left, right, (((0,), (0,)), ((), ())), preferred_element_type=F32)


def silu_slope(pre_value):
    logistic = jax.nn.sigmoid(pre_value)
    return logistic * (1.0 + pre_value * (1.0 - logistic))


def ring_gather(own, onward, back, size):
    groups = [own]
    ahead = behind = own
    for _ in range(1, size // 2):
        ahead = lax.ppermute(ahead, "expert", onward)
        behind = lax.ppermute(behind, "expert", back)
        groups.append(jnp.concatenate([ahead, behind], axis=0))
    half = own.shape[0] // 2
    low = lax.ppermute(ahead[:half], "expert", onward)
    high = lax.ppermute(behind[half:], "expert", back)
    groups.append(jnp.concatenate([low, high], axis=0))
    return groups


def ring_reduce(parts, onward, back, size):
    rows = parts[0].shape[0]
    half = rows // 2
    steps = size // 2
    far = parts[steps]
    to_ahead = lax.ppermute(far[half:].astype(BF16), "expert", onward)
    to_behind = lax.ppermute(far[:half].astype(BF16), "expert", back)
    for step in range(steps - 1, 0, -1):
        own_behind, own_ahead = parts[step][:rows], parts[step][rows:]
        if step == steps - 1:
            send_ahead = jnp.concatenate(
                [own_ahead[:half], own_ahead[half:] + to_ahead.astype(F32)], axis=0
            )
            send_behind = jnp.concatenate(
                [own_behind[:half] + to_behind.astype(F32), own_behind[half:]], axis=0
            )
        else:
            send_ahead = own_ahead + to_ahead.astype(F32)
            send_behind = own_behind + to_behind.astype(F32)
        to_ahead = lax.ppermute(send_ahead.astype(BF16), "expert", onward)
        to_behind = lax.ppermute(send_behind.astype(BF16), "expert", back)
    return (parts[0] + to_ahead.astype(F32) + to_behind.astype(F32)).astype(BF16)


def per_device(tokens, routes, gates, w_in, w_out, cotangent):
    size = lax.axis_size("expert")
    n_dp = lax.axis_size("dp")
    rows, half_width = tokens.shape
    experts = size * w_in.shape[0]
    core = lax.axis_index("tensor")
    place = lax.axis_index("expert")
    order = ring_order(size)
    onward = [(order[i], order[(i + 1) % size]) for i in range(size)]
    back = [(b, a) for a, b in onward]
    steps = size // 2

    gate_table = jnp.sum(
        jnp.where(
            routes.T[None, :, :] == jnp.arange(experts, dtype=jnp.int32)[:, None, None],
            gates.T[None, :, :],
            0.0,
        ),
        axis=1,
    )
    gate_recv = lax.all_to_all(gate_table, "expert", split_axis=0, concat_axis=0, tiled=True)
    position = jnp.where(place % 2 == 0, place // 2, size - 1 - place // 2)
    ring_table = jnp.array(order, dtype=jnp.int32)
    offsets = [0]
    for step in range(1, steps):
        offsets += [-step, step]
    offsets.append(steps)
    sources = ring_table[(position + jnp.array(offsets, dtype=jnp.int32)) % size]
    gate_rel = gate_recv[sources].reshape(size * rows, 1)

    def columns(weights, which):
        return lax.dynamic_slice_in_dim(weights, which * half_width, half_width, axis=1)

    in_mine, in_other = columns(w_in[0], core), columns(w_in[0], 1 - core)
    out_mine, out_other = columns(w_out[0], core), columns(w_out[0], 1 - core)
    in_cols = swap_cores(in_other)
    out_cols = swap_cores(out_other)

    tok_groups = ring_gather(tokens, onward, back, size)
    cot_groups = ring_gather(cotangent, onward, back, size)

    mixed_parts, back_parts, dots, pre_grads, gated, tok_other, cot_other = [], [], [], [], [], [], []
    start = 0
    for tok, cot in zip(tok_groups, cot_groups):
        count = tok.shape[0]
        gate = gate_rel[start : start + count]
        start += count
        tok_o, cot_o = swap_cores(tok), swap_cores(cot)
        pre_value = rows_by_units(tok, in_mine) + rows_by_units(tok_o, in_other)
        hidden = jax.nn.silu(pre_value).astype(BF16).astype(F32)
        gated_hidden = (gate * hidden).astype(BF16)
        mixed_parts.append(
            rows_by_width(gated_hidden, out_mine) + rows_by_width(swap_cores(gated_hidden), out_cols)
        )
        cot_units = rows_by_units(cot, out_mine) + rows_by_units(cot_o, out_other)
        grad_pre = (gate * cot_units * silu_slope(pre_value)).astype(BF16)
        dots.append(jnp.sum(hidden * cot_units, axis=1))
        back_parts.append(
            rows_by_width(grad_pre, in_mine) + rows_by_width(swap_cores(grad_pre), in_cols)
        )
        pre_grads.append(grad_pre)
        gated.append(gated_hidden)
        tok_other.append(tok_o)
        cot_other.append(cot_o)

    def weight_grad(left, mine, other):
        left, mine, other = (jnp.concatenate(v, axis=0) for v in (left, mine, other))
        part_mine, part_other = over_rows(left, mine), over_rows(left, other)
        part = jnp.concatenate(
            [
                jnp.where(core == 0, part_mine, part_other),
                jnp.where(core == 0, part_other, part_mine),
            ],
            axis=1,
        )
        width = part.shape[1] // n_dp
        group = lax.axis_index("dp")

        def piece(which):
            return lax.dynamic_slice_in_dim(part, which * width, width, axis=1)

        total = piece(group)
        for shift in range(1, n_dp):
            sent = piece((group + shift) % n_dp).astype(BF16)
            total = total + lax.ppermute(
                sent, "dp", [(i, (i + shift) % n_dp) for i in range(n_dp)]
            ).astype(F32)
        return total[None]

    grad_out = weight_grad(gated, cot_groups, cot_other)
    grad_in = weight_grad(pre_grads, tok_groups, tok_other)
    mixed = ring_reduce(mixed_parts, onward, back, size)
    grad_tokens = ring_reduce(back_parts, onward, back, size)

    dot_rel = jnp.concatenate(dots, axis=0)
    dot_rel = (dot_rel + swap_cores(dot_rel)).reshape(size, rows)
    dot_send = jnp.zeros((size, rows), F32).at[sources].set(dot_rel)
    dot_recv = lax.all_to_all(dot_send, "expert", split_axis=0, concat_axis=0, tiled=True)
    grad_gates = jnp.sum(
        jnp.where(
            routes[:, :, None] == jnp.arange(experts, dtype=jnp.int32)[None, None, :],
            dot_recv.T[:, None, :],
            0.0,
        ),
        axis=2,
    )
    return (mixed, grad_tokens, grad_gates, grad_in, grad_out)


def solution(mesh):
    placed = (
        P(("dp", "expert"), "tensor"),
        P(("dp", "expert"), None),
        P(("dp", "expert"), None),
        P("expert", "tensor", None),
        P("expert", "tensor", None),
        P(("dp", "expert"), "tensor"),
    )
    return jax.shard_map(
        per_device,
        mesh=mesh,
        in_specs=placed,
        out_specs=(
            P(("dp", "expert"), "tensor"),
            P(("dp", "expert"), "tensor"),
            P(("dp", "expert"), None),
            P("expert", "tensor", "dp"),
            P("expert", "tensor", "dp"),
        ),
        check_vma=False,
    )
```

```python
import functools

import jax
import jax.numpy as jnp
from jax import lax
from jax.experimental import pallas as pl
from jax.experimental.pallas import tpu as pltpu
from jax.sharding import PartitionSpec as P

BF16 = jnp.bfloat16
F32 = jnp.float32
VMEM_LIMIT = 32 * 1024 * 1024


def ring_order(count):
    if count % 2:
        return list(range(count))
    return list(range(0, count, 2)) + list(range(count - 1, 0, -2))


def swap_cores(value):
    return lax.ppermute(value, "tensor", [(0, 1), (1, 0)])


def tied(values, others):
    out = lax.optimization_barrier((tuple(values), tuple(others)))
    return out[0]


def dot_units(rows, weights):
    return lax.dot_general(rows, weights, (((1,), (1,)), ((), ())), preferred_element_type=F32)


def dot_width(rows, weights):
    return lax.dot_general(rows, weights, (((1,), (0,)), ((), ())), preferred_element_type=F32)


def dot_rows(left, right):
    return lax.dot_general(left, right, (((0,), (0,)), ((), ())), preferred_element_type=F32)


def call(kernel, out_shape, operands, flops, scalars):
    moved = sum(v.size * v.dtype.itemsize for v in operands) + sum(
        v.size * v.dtype.itemsize for v in out_shape
    )
    return pl.pallas_call(
        kernel,
        out_shape=out_shape,
        in_specs=[pl.BlockSpec(memory_space=pltpu.SMEM)]
        + [pl.BlockSpec(memory_space=pltpu.VMEM)] * len(operands),
        out_specs=[pl.BlockSpec(memory_space=pltpu.VMEM)] * len(out_shape),
        compiler_params=pltpu.CompilerParams(vmem_limit_bytes=VMEM_LIMIT),
        cost_estimate=pl.CostEstimate(flops=flops, bytes_accessed=moved, transcendentals=0),
    )(scalars, *operands)


def stacked(refs):
    return jnp.concatenate([ref[...] for ref in refs], axis=0) if len(refs) > 1 else refs[0][...]


def column_of(row):
    count = row.shape[1]
    across = lax.broadcasted_iota(jnp.int32, (count, count), 0)
    along = lax.broadcasted_iota(jnp.int32, (count, count), 1)
    return jnp.sum(jnp.where(across == along, row, 0.0), axis=1, keepdims=True)


def row_of(column):
    count = column.shape[0]
    across = lax.broadcasted_iota(jnp.int32, (count, count), 0)
    along = lax.broadcasted_iota(jnp.int32, (count, count), 1)
    return jnp.sum(jnp.where(across == along, column, 0.0), axis=0, keepdims=True)


def halves_of(w_ref, core):
    width = w_ref.shape[1] // 2
    mine = w_ref[:, pl.ds(pl.multiple_of(core * width, width), width)]
    other = w_ref[:, pl.ds(pl.multiple_of((1 - core) * width, width), width)]
    return mine, other


def forward_kernel(n_rows, n_gates, scalars, *refs):
    mine, other = refs[:n_rows], refs[n_rows : 2 * n_rows]
    tables = refs[2 * n_rows : 2 * n_rows + n_gates]
    w_ref, hidden_ref, gated_ref, slope_ref = refs[2 * n_rows + n_gates :]
    w_mine, w_other = halves_of(w_ref, scalars[0])
    gate = jnp.concatenate([column_of(t[pl.ds(scalars[1], 1), :]) for t in tables], axis=0)
    pre = dot_units(stacked(mine), w_mine) + dot_units(stacked(other), w_other)
    logistic = 1.0 / (1.0 + jnp.exp(-pre))
    hidden = (pre * logistic).astype(BF16)
    hidden_ref[...] = hidden
    gated_ref[...] = (gate * hidden.astype(F32)).astype(BF16)
    slope_ref[...] = gate * (logistic * (1.0 + pre * (1.0 - logistic)))


def backward_kernel(n_rows, scalars, *refs):
    mine, other = refs[:n_rows], refs[n_rows : 2 * n_rows]
    w_ref, hidden_ref, slope_ref, grad_ref, dots_ref = refs[2 * n_rows :]
    w_mine, w_other = halves_of(w_ref, scalars[0])
    units = dot_units(stacked(mine), w_mine) + dot_units(stacked(other), w_other)
    grad_ref[...] = (slope_ref[...] * units).astype(BF16)
    sums = jnp.sum(hidden_ref[...].astype(F32) * units, axis=1, keepdims=True)
    count = dots_ref.shape[1]
    for i in range(dots_ref.shape[0]):
        dots_ref[i : i + 1, :] = row_of(sums[i * count : (i + 1) * count])


def return_kernel(kind, scalars, *refs):
    mine_ref, other_ref, w_ref, w_cols_ref = refs[:4]
    width = w_cols_ref.shape[1]
    w_mine = w_ref[:, pl.ds(pl.multiple_of(scalars[0] * width, width), width)]
    part = dot_width(mine_ref[...], w_mine) + dot_width(other_ref[...], w_cols_ref[...])
    count = part.shape[0] // 2
    if kind == "far":
        behind_ref, ahead_ref = refs[4:]
        behind_ref[...] = part[:count].astype(BF16)
        ahead_ref[...] = part[count:].astype(BF16)
    elif kind == "join":
        half = count // 2
        from_ahead, from_behind, behind_ref, ahead_ref = refs[4:]
        behind_ref[:half, :] = (part[:half] + from_ahead[...].astype(F32)).astype(BF16)
        behind_ref[half:, :] = part[half:count].astype(BF16)
        ahead_ref[:half, :] = part[count : count + half].astype(BF16)
        ahead_ref[half:, :] = (part[count + half :] + from_behind[...].astype(F32)).astype(BF16)
    elif kind == "add":
        from_ahead, from_behind, behind_ref, ahead_ref = refs[4:]
        behind_ref[...] = (part[:count] + from_ahead[...].astype(F32)).astype(BF16)
        ahead_ref[...] = (part[count:] + from_behind[...].astype(F32)).astype(BF16)
    else:
        from_ahead, from_behind, out_ref = refs[4:]
        total = part + from_ahead[...].astype(F32) + from_behind[...].astype(F32)
        out_ref[...] = total.astype(BF16)


def weight_kernel(n_left, n_right, scalars, *refs):
    left = refs[:n_left]
    mine = refs[n_left : n_left + n_right]
    other = refs[n_left + n_right : n_left + 2 * n_right]
    out_ref = refs[-1]

    @pl.when(scalars[0] == 0)
    def _():
        out_ref[...] = dot_rows(stacked(left), stacked(mine)).astype(out_ref.dtype)

    @pl.when(scalars[0] != 0)
    def _():
        out_ref[...] = dot_rows(stacked(left), stacked(other)).astype(out_ref.dtype)


def per_device(tokens, routes, gates, w_in, w_out, cotangent):
    size = lax.axis_size("expert")
    n_dp = lax.axis_size("dp")
    rows, half_width = tokens.shape
    half = rows // 2
    experts = size * w_in.shape[0]
    core = lax.axis_index("tensor")
    place = lax.axis_index("expert")
    group = lax.axis_index("dp")
    order = ring_order(size)
    onward_pairs = [(order[i], order[(i + 1) % size]) for i in range(size)]
    back_pairs = [(b, a) for a, b in onward_pairs]
    steps = size // 2
    scalars = jnp.stack([core, place]).astype(jnp.int32)
    w_in, w_out = w_in[0], w_out[0]
    units = w_in.shape[0]

    def onward(value):
        return lax.ppermute(value, "expert", onward_pairs)

    def back(value):
        return lax.ppermute(value, "expert", back_pairs)

    def other_columns(weights):
        return lax.dynamic_slice_in_dim(weights, (1 - core) * half_width, half_width, axis=1)

    table = jnp.sum(
        jnp.where(
            routes.T[None, :, :] == jnp.arange(experts, dtype=jnp.int32)[:, None, None],
            gates.T[None, :, :],
            0.0,
        ),
        axis=1,
    )

    def forward(mine, other, tables):
        count = sum(v.shape[0] for v in mine)
        shape = (count, units)
        return call(
            functools.partial(forward_kernel, len(mine), len(tables)),
            [
                jax.ShapeDtypeStruct(shape, BF16),
                jax.ShapeDtypeStruct(shape, BF16),
                jax.ShapeDtypeStruct(shape, F32),
            ],
            [*mine, *other, *tables, w_in],
            4 * count * units * half_width,
            scalars,
        )

    def backward(mine, other, hidden, slope):
        count = sum(v.shape[0] for v in mine)
        return call(
            functools.partial(backward_kernel, len(mine)),
            [
                jax.ShapeDtypeStruct((count, units), BF16),
                jax.ShapeDtypeStruct((count // rows, rows), F32),
            ],
            [*mine, *other, w_out, hidden, slope],
            4 * count * units * half_width,
            scalars,
        )

    def returned(kind, mine, other, weights, cols, arrived):
        count = mine.shape[0]
        if kind == "own":
            shapes = [(rows, half_width)]
        elif kind == "far":
            shapes = [(half, half_width)] * 2
        else:
            shapes = [(rows, half_width)] * 2
        return call(
            functools.partial(return_kernel, kind),
            [jax.ShapeDtypeStruct(s, BF16) for s in shapes],
            [mine, other, weights, cols, *arrived],
            4 * count * units * half_width,
            scalars,
        )

    def weight_part(which, left, mine, other, dtype):
        return call(
            functools.partial(weight_kernel, len(left), len(mine)),
            [jax.ShapeDtypeStruct((units, half_width), dtype)],
            [*left, *mine, *other],
            2 * size * rows * units * half_width,
            jnp.reshape(which, (1,)).astype(jnp.int32),
        )[0]

    tok_in = (onward(tokens), back(tokens))
    cot_in = (onward(cotangent), back(cotangent))
    table_in = (onward(table), back(table))
    in_cols = swap_cores(other_columns(w_in))
    out_cols = swap_cores(other_columns(w_out))

    def take_tokens(mine, tables):
        other = tuple(swap_cores(v) for v in mine)
        hidden, gated, slope = forward(mine, other, tables)
        return {
            "tok": (mine, other),
            "hidden": hidden,
            "slope": slope,
            "gated": gated,
            "gated_other": swap_cores(gated),
        }

    def take_cotangent(item, mine):
        other = tuple(swap_cores(v) for v in mine)
        grad, dots = backward(mine, other, item["hidden"], item["slope"])
        item["cot"] = (mine, other)
        item["grad"] = grad
        item["grad_other"] = swap_cores(grad)
        item["dots"] = dots + swap_cores(dots)
        return item

    items = [take_tokens((tokens,), (table,))]
    take_cotangent(items[0], (cotangent,))
    last = (items[0]["grad"], items[0]["gated"])
    for step in range(1, steps + 1):
        tok_now, cot_now, table_now = tok_in, cot_in, table_in
        tok_now = tied(tok_now, last)
        if step < steps - 1:
            tok_in = (onward(tok_now[0]), back(tok_now[1]))
            table_in = (onward(table_now[0]), back(table_now[1]))
        elif step == steps - 1:
            tok_in = (onward(tok_now[0][:half]), back(tok_now[1][half:]))
            table_in = (onward(table_now[0]),)
        item = take_tokens(tok_now, table_now)
        cot_now = tied(cot_now, (item["gated"],))
        if step < steps - 1:
            cot_in = (onward(cot_now[0]), back(cot_now[1]))
        elif step == steps - 1:
            cot_in = (onward(cot_now[0][:half]), back(cot_now[1][half:]))
        take_cotangent(item, cot_now)
        last = (item["grad"],)
        items.append(item)

    row_mask = jnp.arange(experts, dtype=jnp.int32)[:, None] == place

    def dots_table(row):
        return jnp.where(row_mask, row[None, :], 0.0)

    far = items[steps]
    to_behind, to_ahead = returned("far", far["gated"], far["gated_other"], w_out, out_cols, ())
    mixed_in = (back(to_behind), onward(to_ahead))
    to_behind, to_ahead = returned("far", far["grad"], far["grad_other"], w_in, in_cols, ())
    back_in = (back(to_behind), onward(to_ahead))
    dots_in = (None, onward(dots_table(far["dots"][0])))

    gated = [v["gated"] for v in items]
    grads = [v["grad"] for v in items]
    toks = [[x for v in items for x in v["tok"][i]] for i in (0, 1)]
    cots = [[x for v in items for x in v["cot"][i]] for i in (0, 1)]

    def weight_sent(left, right):
        if n_dp == 2:
            sent = weight_part((1 - group) != core, left, *right, BF16)
            return lax.ppermute(sent, "dp", [(0, 1), (1, 0)])
        part_mine = weight_part(jnp.int32(0), left, *right, F32)
        part_other = weight_part(jnp.int32(1), left, *right, F32)
        part = jnp.concatenate(
            [
                jnp.where(core == 0, part_mine, part_other),
                jnp.where(core == 0, part_other, part_mine),
            ],
            axis=1,
        )
        width = part.shape[1] // n_dp
        pieces = [
            lax.dynamic_slice_in_dim(part, ((group + shift) % n_dp) * width, width, axis=1)
            for shift in range(n_dp)
        ]
        total = pieces[0]
        for shift in range(1, n_dp):
            pairs = [(i, (i + shift) % n_dp) for i in range(n_dp)]
            total = total + lax.ppermute(pieces[shift].astype(BF16), "dp", pairs).astype(F32)
        return total

    def weight_total(left, right, arrived):
        if n_dp != 2:
            return arrived[None]
        own = weight_part(group != core, left, *right, F32)
        return (own + arrived.astype(F32))[None]

    out_arrived = weight_sent(gated, cots)
    in_arrived = weight_sent(grads, toks)

    for step in range(steps - 1, 0, -1):
        item = items[step]
        kind = "join" if step == steps - 1 else "add"
        to_behind, to_ahead = returned(
            kind, item["gated"], item["gated_other"], w_out, out_cols, mixed_in
        )
        mixed_in = (back(to_behind), onward(to_ahead))
        back_in = tied(back_in, (to_behind, to_ahead))
        to_behind, to_ahead = returned(
            kind, item["grad"], item["grad_other"], w_in, in_cols, back_in
        )
        back_in = (back(to_behind), onward(to_ahead))
        mixed_in = tied(mixed_in, (to_behind, to_ahead))
        table_behind, table_ahead = dots_table(item["dots"][0]), dots_table(item["dots"][1])
        if dots_in[0] is not None:
            table_behind = table_behind + dots_in[0]
        table_ahead = table_ahead + dots_in[1]
        dots_in = (back(table_behind), onward(table_ahead))

    own = items[0]
    mixed = returned("own", own["gated"], own["gated_other"], w_out, out_cols, mixed_in)[0]
    grad_tokens = returned("own", own["grad"], own["grad_other"], w_in, in_cols, back_in)[0]
    grad_out = weight_total(gated, cots, out_arrived)
    grad_in = weight_total(grads, toks, in_arrived)
    dots = dots_table(own["dots"][0]) + dots_in[0] + dots_in[1]
    grad_gates = jnp.sum(
        jnp.where(
            routes[:, :, None] == jnp.arange(experts, dtype=jnp.int32)[None, None, :],
            dots.T[:, None, :],
            0.0,
        ),
        axis=2,
    )
    return (mixed, grad_tokens, grad_gates, grad_in, grad_out)


def solution(mesh):
    placed = (
        P(("dp", "expert"), "tensor"),
        P(("dp", "expert"), None),
        P(("dp", "expert"), None),
        P("expert", "tensor", None),
        P("expert", "tensor", None),
        P(("dp", "expert"), "tensor"),
    )
    return jax.shard_map(
        per_device,
        mesh=mesh,
        in_specs=placed,
        out_specs=(
            P(("dp", "expert"), "tensor"),
            P(("dp", "expert"), "tensor"),
            P(("dp", "expert"), None),
            P("expert", "tensor", "dp"),
            P("expert", "tensor", "dp"),
        ),
        check_vma=False,
    )
```

```python
import functools

import jax
import jax.numpy as jnp
from jax import lax
from jax.experimental import pallas as pl
from jax.experimental.pallas import tpu as pltpu
from jax.sharding import PartitionSpec as P

BF16 = jnp.bfloat16
F32 = jnp.float32
VMEM_LIMIT = 16 * 1024 * 1024
LANES = 128
EXTRA = 16


def ring_order(count):
    if count % 2:
        return list(range(count))
    return list(range(0, count, 2)) + list(range(count - 1, 0, -2))


def swap_cores(value, name):
    with jax.named_scope("swap_" + name):
        return lax.ppermute(value, "tensor", [(0, 1), (1, 0)])


def tied(values, others):
    return lax.optimization_barrier((tuple(values), tuple(others)))[0]


def dot_units(rows, weights):
    return lax.dot_general(rows, weights, (((1,), (1,)), ((), ())), preferred_element_type=F32)


def dot_width(rows, weights):
    return lax.dot_general(rows, weights, (((1,), (0,)), ((), ())), preferred_element_type=F32)


def dot_rows(left, right):
    return lax.dot_general(left, right, (((0,), (0,)), ((), ())), preferred_element_type=F32)


def call(kernel, out_shape, operands, scalars, work=4 * 10**9):
    return pl.pallas_call(
        kernel,
        out_shape=out_shape,
        in_specs=[pl.BlockSpec(memory_space=pltpu.SMEM)]
        + [pl.BlockSpec(memory_space=pltpu.VMEM)] * len(operands),
        out_specs=[pl.BlockSpec(memory_space=pltpu.VMEM)] * len(out_shape),
        compiler_params=pltpu.CompilerParams(vmem_limit_bytes=VMEM_LIMIT),
        cost_estimate=pl.CostEstimate(flops=work, bytes_accessed=0, transcendentals=0),
    )(scalars, *operands)


def picked(core, first, second):
    return jnp.where(core == 0, first, second)


def diagonal(count):
    across = lax.broadcasted_iota(jnp.int32, (count, count), 0)
    along = lax.broadcasted_iota(jnp.int32, (count, count), 1)
    return across == along


def column_of(row):
    return jnp.sum(jnp.where(diagonal(row.shape[1]), row, 0.0), axis=1, keepdims=True)


def row_of(column):
    return jnp.sum(jnp.where(diagonal(column.shape[0]), column, 0.0), axis=0, keepdims=True)


def pieces_of(value):
    high = value.astype(BF16).astype(F32)
    middle = (value - high).astype(BF16).astype(F32)
    return high, middle, value - high - middle


def prepare_kernel(scalars, local_ref, arrived_ref, mine_ref, other_ref):
    core = scalars[0]
    units, width = local_ref.shape[0], local_ref.shape[1] // 2
    for ref, where in ((local_ref, core), (arrived_ref, 1 - core)):
        at = pl.ds(pl.multiple_of(where * units, units), units)
        mine_ref[at, :] = ref[:, pl.ds(pl.multiple_of(core * width, width), width)]
        other_ref[at, :] = ref[:, pl.ds(pl.multiple_of((1 - core) * width, width), width)]


def stacked(values):
    return jnp.concatenate(values, axis=0) if len(values) > 1 else values[0]


def units_of(core, rows_refs, w_ref, w_other_ref):
    mine = stacked([picked(core, f[...], s[...]) for f, s, _ in rows_refs])
    other = stacked([a[...] for _, _, a in rows_refs])
    return dot_units(mine, w_ref[...]) + dot_units(other, w_other_ref[...])


def forward_kernel(slots, with_next, scalars, *refs):
    if with_next:
        refs = give_next(scalars[0], refs)
    rows_refs = [refs[3 * i : 3 * i + 3] for i in range(len(slots))]
    gates_ref, w_ref, w_other_ref, hidden_ref, gated_ref, slope_ref = refs[3 * len(slots) :]
    core = scalars[0]
    columns = []
    for slot, piece in zip(slots, rows_refs):
        count = piece[2].shape[0]
        gate = column_of(gates_ref[pl.ds(scalars[2 + slot], 1), :])
        if count < gate.shape[0]:
            gate = picked(core, gate[:count], gate[count:])
        columns.append(gate)
    gate = stacked(columns)
    pre = units_of(core, rows_refs, w_ref, w_other_ref)
    logistic = 1.0 / (1.0 + jnp.exp(-pre))
    hidden = (pre * logistic).astype(BF16)
    hidden_ref[...] = hidden
    gated_ref[...] = (gate * hidden.astype(F32)).astype(BF16)
    slope_ref[...] = gate * (logistic * (1.0 + pre * (1.0 - logistic)))


def give_next(core, refs):
    refs[-1][...] = picked(core, refs[1][...], refs[0][...])
    return refs[2:-1]


def backward_kernel(pieces, with_next, scalars, *refs):
    if with_next:
        refs = give_next(scalars[0], refs)
    rows_refs = [refs[3 * i : 3 * i + 3] for i in range(pieces)]
    w_ref, w_other_ref, hidden_ref, gated_ref, slope_ref, out_ref = refs[3 * pieces :]
    count, units = hidden_ref.shape
    wide = units_of(scalars[0], rows_refs, w_ref, w_other_ref)
    out_ref[:, :units] = gated_ref[...]
    out_ref[:, units : 2 * units] = (slope_ref[...] * wide).astype(BF16)
    sums = jnp.sum(hidden_ref[...].astype(F32) * wide, axis=1, keepdims=True)
    lane = lax.broadcasted_iota(jnp.int32, (count, LANES), 1)
    kept = jnp.zeros((count, LANES), F32)
    for i, piece in enumerate(pieces_of(sums)):
        kept = jnp.where(lane == i, piece, kept)
    out_ref[:, 2 * units :] = kept.astype(BF16)


def dots_rows(expert, dots, start, rows, width, experts):
    count = dots.shape[0]
    row = row_of(dots)
    if count < rows:
        blank = jnp.zeros((1, count), F32)
        row = jnp.concatenate([row, blank] if start == 0 else [blank, row], axis=1)
    per_row = width // rows
    deep = -(-experts // per_row)
    line = lax.broadcasted_iota(jnp.int32, (EXTRA, width), 0)
    lane = lax.broadcasted_iota(jnp.int32, (EXTRA, width), 1)
    chosen = lane // rows == lax.rem(expert, per_row)
    out = jnp.zeros((EXTRA, width), F32)
    for i, piece in enumerate(pieces_of(row)):
        spread = jnp.concatenate([piece] * per_row, axis=1)
        out = jnp.where(chosen & (line == i * deep + expert // per_row), spread, out)
    return out


def return_kernel(kind, at, first_row, count, experts, rows, scalars, mine_ref, arrived_ref, w_ref, *refs):
    core, expert = scalars[0], scalars[1]
    units, width = w_ref.shape
    lines = slice(first_row, first_row + count)
    mine, arrived = mine_ref[lines, at : at + units], arrived_ref[lines, at : at + units]
    both = jnp.concatenate([picked(core, mine, arrived), picked(core, arrived, mine)], axis=0)
    part = dot_width(both, w_ref[...])
    with_dots = at > 0
    extra = [None, None]
    if with_dots:
        mine = jnp.sum(mine_ref[lines, 2 * units :].astype(F32), axis=1, keepdims=True)
        arrived = jnp.sum(arrived_ref[lines, 2 * units :].astype(F32), axis=1, keepdims=True)
        dots = [picked(core, mine, arrived), picked(core, arrived, mine)]
        starts = (0, count if count < rows else 0)
        extra = [
            dots_rows(expert, d, start, rows, width, experts) for d, start in zip(dots, starts)
        ]
    if kind == "far":
        for i, out_ref in enumerate(refs):
            out_ref[:count, :] = part[i * count : (i + 1) * count].astype(BF16)
            if with_dots:
                out_ref[count:, :] = extra[i].astype(BF16)
        return
    from_ahead, from_behind = refs[:2]
    if kind == "own":
        total = part + from_ahead[:rows, :].astype(F32) + from_behind[:rows, :].astype(F32)
        if not with_dots:
            refs[2][...] = total.astype(BF16)
            return
        routes_ref, out_ref, gates_ref = refs[2:]
        out_ref[...] = total.astype(BF16)
        table = extra[0] + extra[1]
        table = table + from_ahead[rows:, :].astype(F32) + from_behind[rows:, :].astype(F32)
        per_row = width // rows
        deep = -(-experts // per_row)
        routes = routes_ref[...]
        grads = jnp.zeros(routes.shape, F32)
        for e in range(experts):
            lanes = slice((e % per_row) * rows, (e % per_row + 1) * rows)
            line = e // per_row
            row = sum(table[i * deep + line : i * deep + line + 1, lanes] for i in range(3))
            grads = jnp.where(routes == e, column_of(row), grads)
        gates_ref[...] = grads
        return
    behind_ref, ahead_ref = refs[2:]
    behind, ahead = part[:count], part[count:]
    if kind == "join":
        half = count // 2
        behind_ref[:half, :] = (behind[:half] + from_ahead[:half, :].astype(F32)).astype(BF16)
        behind_ref[half:count, :] = behind[half:].astype(BF16)
        ahead_ref[:half, :] = ahead[:half].astype(BF16)
        ahead_ref[half:count, :] = (ahead[half:] + from_behind[:half, :].astype(F32)).astype(BF16)
    else:
        half = count
        behind_ref[:count, :] = (behind + from_ahead[:count, :].astype(F32)).astype(BF16)
        ahead_ref[:count, :] = (ahead + from_behind[:count, :].astype(F32)).astype(BF16)
    if with_dots:
        behind_ref[count:, :] = (extra[0] + from_ahead[half:, :].astype(F32)).astype(BF16)
        ahead_ref[count:, :] = (extra[1] + from_behind[half:, :].astype(F32)).astype(BF16)


def weight_kernel(pieces, at, scalars, *refs):
    core = scalars[0]
    lefts, rights = [], []
    mine_ref, other_ref = refs[-2:]
    units = mine_ref.shape[0]
    taken = 0
    for count in pieces:
        mine, arrived = refs[taken : taken + 2]
        firsts = refs[taken + 2 : taken + 2 + count]
        seconds = refs[taken + 2 + count : taken + 2 + 2 * count]
        taken += 2 + 2 * count
        own, came = mine[:, at : at + 2 * units], arrived[:, at : at + 2 * units]
        lefts += [picked(core, own, came), picked(core, came, own)]
        rights += [*firsts, *seconds]
    part = dot_rows(stacked(lefts), stacked([v[...] for v in rights]))
    mine_ref[...] = picked(core, part[:units], part[units:]).astype(BF16)
    other_ref[...] = picked(core, part[units:], part[:units]).astype(BF16)


def add_kernel(scalars, *refs):
    first, second, came, first_out, second_out = refs
    count = first.shape[0]
    first_out[...] = first[...].astype(F32) + came[:count, :].astype(F32)
    second_out[...] = second[...].astype(F32) + came[count:, :].astype(F32)


def send_kernel(scalars, first_mine, first_came, second_mine, second_came, sent, first, second):
    count = first.shape[0]

    @pl.when(scalars[0] == 0)
    def _():
        sent[:count, :] = first_came[...]
        sent[count:, :] = second_came[...]
        first[...] = first_mine[...]
        second[...] = second_mine[...]

    @pl.when(scalars[0] != 0)
    def _():
        sent[:count, :] = first_mine[...]
        sent[count:, :] = second_mine[...]
        first[...] = first_came[...]
        second[...] = second_came[...]


def per_device(tokens, routes, gates, w_in, w_out, cotangent):
    size = lax.axis_size("expert")
    n_dp = lax.axis_size("dp")
    rows, width = tokens.shape
    half = rows // 2
    experts = size * w_in.shape[0]
    core = lax.axis_index("tensor")
    place = lax.axis_index("expert")
    group = lax.axis_index("dp")
    order = ring_order(size)
    onward_pairs = [(order[i], order[(i + 1) % size]) for i in range(size)]
    back_pairs = [(b, a) for a, b in onward_pairs]
    steps = size // 2
    w_in, w_out = w_in[0], w_out[0]
    local_units = w_in.shape[0]
    units = 2 * local_units

    def both_ways(forth_value, back_value, name):
        with jax.named_scope("onward_" + name):
            forth = lax.ppermute(forth_value, "expert", onward_pairs)
        with jax.named_scope("back_" + name):
            return forth, lax.ppermute(back_value, "expert", back_pairs)

    table = jnp.sum(
        jnp.where(
            routes.T[None, :, :] == jnp.arange(experts, dtype=jnp.int32)[:, None, None],
            gates.T[None, :, :],
            0.0,
        ),
        axis=1,
    )
    gate_rows = lax.all_to_all(table, "expert", split_axis=0, concat_axis=0, tiled=True)

    position = jnp.where(place % 2 == 0, place // 2, size - 1 - place // 2)
    shifts = jnp.array([0, *range(1, steps), steps], dtype=jnp.int32)
    at_ring = (position + picked(core, -shifts, shifts) + size) % size
    sources = jnp.where(at_ring < steps, 2 * at_ring, 2 * (size - 1 - at_ring) + 1)
    scalars = jnp.concatenate([jnp.stack([core, place]), sources]).astype(jnp.int32)

    def next_shape(following):
        return [jax.ShapeDtypeStruct(v.shape, BF16) for v in following[:1]]

    def forward(slots, pieces, following=()):
        count = sum(p[2].shape[0] for p in pieces)
        shape = (count, units)
        return call(
            functools.partial(forward_kernel, slots, len(following) > 0),
            [
                jax.ShapeDtypeStruct(shape, BF16),
                jax.ShapeDtypeStruct(shape, BF16),
                jax.ShapeDtypeStruct(shape, F32),
                *next_shape(following),
            ],
            [*following, *(v for p in pieces for v in p), gate_rows, *in_all],
            scalars,
        )

    def backward(pieces, hidden, gated, slope, following=()):
        count = hidden.shape[0]
        return call(
            functools.partial(backward_kernel, len(pieces), len(following) > 0),
            [jax.ShapeDtypeStruct((count, 2 * units + LANES), BF16), *next_shape(following)],
            [*following, *(v for p in pieces for v in p), *out_all, hidden, gated, slope],
            scalars,
        )

    def returned(kind, at, mine, arrived, weights, sums, more=()):
        count = rows if kind in ("join", "add") else half
        first_row = half if kind == "far" and mine.shape[0] > half else 0
        extra = EXTRA if at else 0
        if kind == "own":
            shapes = [jax.ShapeDtypeStruct((rows, width), BF16)]
            if at:
                shapes.append(jax.ShapeDtypeStruct(routes.shape, F32))
        else:
            shapes = [jax.ShapeDtypeStruct((count + extra, width), BF16)] * 2
        return call(
            functools.partial(return_kernel, kind, at, first_row, count, experts, rows),
            shapes,
            [mine, arrived, weights, *sums, *more],
            scalars,
        )

    ring = [both_ways(tokens, tokens, "tok1"), both_ways(cotangent, cotangent, "cot1")]

    def prepared(weights):
        return call(
            prepare_kernel,
            [jax.ShapeDtypeStruct((units, width), BF16)] * 2,
            [weights, swap_cores(weights, "weights")],
            scalars,
        )

    in_all = prepared(w_in)
    out_all = prepared(tied((w_out,), ring[0])[0])

    own_sent = jnp.concatenate(
        [
            lax.dynamic_slice_in_dim(v, (1 - core) * half, half, axis=0)
            for v in (tokens, cotangent)
        ],
        axis=0,
    )

    arrivals, outputs, lefts, lefts_arrived = [], [], [], []
    own_arrived = None
    for turn in range(2 * steps):
        now = ring[turn]
        step = turn // 2 + 1
        name = ("tok", "cot")[turn % 2]
        picked_rows = None
        if 1 <= turn < 2 * steps - 1:
            done = turn - 1
            at_end = turn == 2 * steps - 3
            first, second, other = arrivals[done]
            if done % 2 == 0 and len(lefts) > len(lefts_arrived) + 1:
                index = len(lefts_arrived)
                sent = tied((lefts[index],), outputs[-1])[0]
                lefts_arrived.append(swap_cores(sent, "left" + str(index + 1)))
            elif done % 2 == 1 and lefts_arrived:
                other = tied((other,), lefts_arrived[-1:])[0]
            if at_end:
                other = tied((other,), now)[0]
            pieces = [(first, second, other)]
            following = () if at_end else now
            if done % 2 == 0:
                result = forward((done // 2 + 1,), pieces, following)
            else:
                result = backward(pieces, *outputs[done - 1], following)
                lefts.append(result[0])
            if not at_end:
                *result, picked_rows = result
                now = tied(now, (picked_rows,))
            outputs.append(result)
        if picked_rows is None:
            picked_rows = picked(core, now[1], now[0])
        if step < steps - 1:
            ring.append(both_ways(now[0], now[1], name + str(step + 1)))
        elif step == steps - 1:
            ring.append(both_ways(ring[turn][0][:half], ring[turn][1][half:], name + str(step + 1)))
        if turn == 1:
            both = swap_cores(jnp.concatenate([picked_rows, own_sent], axis=0), name + str(step))
            other, own_arrived = both[:rows], both[rows:]
        else:
            other = swap_cores(picked_rows, name + str(step))
        arrivals.append((*now, other))
    tok_pieces = [(tokens[:half], tokens[half:], own_arrived[:half]), arrivals[2 * steps - 2]]
    cot_pieces = [(cotangent[:half], cotangent[half:], own_arrived[half:]), arrivals[2 * steps - 1]]
    tok_pieces[1] = tied(tok_pieces[1], (*lefts, *lefts_arrived))
    hidden, gated, slope = forward((0, steps), tok_pieces)
    gated_arrived = swap_cores(gated, "gated")
    ends = backward(cot_pieces, hidden, gated, slope)[0]
    ends_arrived = swap_cores(ends, "ends")
    for index in range(len(lefts_arrived), steps - 1):
        sent = tied((lefts[index],), (ends_arrived,))[0]
        lefts_arrived.append(swap_cores(sent, "left" + str(index + 1)))

    sent = returned("far", 0, gated, gated_arrived, out_all[0], ())
    mixed_in = both_ways(sent[1], sent[0], "mixed")[::-1]
    sent = returned("far", units, ends, ends_arrived, in_all[0], ())
    back_in = both_ways(sent[1], sent[0], "grad")[::-1]

    def weight_part(at, which, after):
        operands = []
        for s in range(steps - 1):
            operands += [lefts[s], lefts_arrived[s], *arrivals[2 * s + which][:2]]
        pieces = (tok_pieces, cot_pieces)[which]
        operands += [ends, tied((ends_arrived,), after)[0]]
        operands += [p[0] for p in pieces] + [p[1] for p in pieces]
        return call(
            functools.partial(weight_kernel, [1] * (steps - 1) + [2], at),
            [jax.ShapeDtypeStruct((local_units, width), BF16)] * 2,
            operands,
            scalars,
        )

    out_mine, out_other = weight_part(0, 1, sent)
    out_other = swap_cores(out_other, "grad_out")
    in_mine, in_other = weight_part(units, 0, (out_mine,))
    in_other = swap_cores(in_other, "grad_in")
    if n_dp == 2:
        away = jnp.reshape(jnp.where(group == core, 0, 1), (1,)).astype(jnp.int32)
        parts_sent, *kept = call(
            send_kernel,
            [jax.ShapeDtypeStruct((2 * local_units, width), BF16)]
            + [jax.ShapeDtypeStruct((local_units, width), BF16)] * 2,
            [out_mine, out_other, in_mine, in_other],
            away,
        )
        parts_came = lax.ppermute(parts_sent, "dp", [(0, 1), (1, 0)])
        after_parts = (parts_sent,)
    else:
        kept, parts_came = [], []
        after_parts = ()
        for mine, arrived in ((out_mine, out_other), (in_mine, in_other)):
            part = jnp.concatenate(
                [picked(core, mine, arrived), picked(core, arrived, mine)], axis=1
            )
            across = part.shape[1] // n_dp
            slices = [
                lax.dynamic_slice_in_dim(part, ((group + shift) % n_dp) * across, across, axis=1)
                for shift in range(n_dp)
            ]
            total = 0.0
            for shift in range(1, n_dp):
                pairs = [(i, (i + shift) % n_dp) for i in range(n_dp)]
                total = total + lax.ppermute(slices[shift], "dp", pairs).astype(F32)
            kept.append(slices[0])
            parts_came.append(total)
        parts_came = jnp.concatenate(parts_came, axis=0)

    first_ties = {steps - 1: ((out_mine,), (in_mine,)), steps - 2: (after_parts, ())}
    for step in range(steps - 1, 0, -1):
        kind = "join" if step == steps - 1 else "add"
        left, left_arrived = lefts[step - 1], lefts_arrived[step - 1]
        mixed_ties, back_ties = first_ties.get(step, ((), ()))
        mixed_in = tied(mixed_in, (*sent, *mixed_ties))
        sent = returned(kind, 0, left, left_arrived, out_all[0], mixed_in)
        mixed_in = both_ways(sent[1], sent[0], "mixed")[::-1]
        back_in = tied(back_in, (*sent, *back_ties))
        sent = returned(kind, units, left, left_arrived, in_all[0], back_in)
        back_in = both_ways(sent[1], sent[0], "grad")[::-1]
    mixed_in = tied(mixed_in, sent)

    mixed = returned("own", 0, ends, ends_arrived, out_all[0], mixed_in)[0]
    grad_tokens, grad_gates = returned(
        "own", units, ends, ends_arrived, in_all[0], back_in, (routes,)
    )

    grad_out, grad_in = call(
        add_kernel,
        [jax.ShapeDtypeStruct(v.shape, F32) for v in kept],
        [*kept, parts_came],
        scalars,
    )
    return (mixed, grad_tokens, grad_gates, grad_in[None], grad_out[None])


def solution(mesh):
    placed = (
        P(("dp", "expert"), "tensor"),
        P(("dp", "expert"), None),
        P(("dp", "expert"), None),
        P("expert", "tensor", None),
        P("expert", "tensor", None),
        P(("dp", "expert"), "tensor"),
    )
    return jax.shard_map(
        per_device,
        mesh=mesh,
        in_specs=placed,
        out_specs=(
            P(("dp", "expert"), "tensor"),
            P(("dp", "expert"), "tensor"),
            P(("dp", "expert"), None),
            P("expert", "tensor", "dp"),
            P("expert", "tensor", "dp"),
        ),
        check_vma=False,
    )
```

```python
import functools

import jax
import jax.numpy as jnp
from jax import lax
from jax.experimental import pallas as pl
from jax.experimental.pallas import tpu as pltpu
from jax.sharding import PartitionSpec as P

BF16 = jnp.bfloat16
F32 = jnp.float32
VMEM_LIMIT = 16 * 1024 * 1024
LANES = 128
EXTRA = 16


def ring_order(count):
    if count % 2:
        return list(range(count))
    return list(range(0, count, 2)) + list(range(count - 1, 0, -2))


def swap_cores(value, name):
    with jax.named_scope("swap_" + name):
        return lax.ppermute(value, "tensor", [(0, 1), (1, 0)])


def tied(values, others):
    return lax.optimization_barrier((tuple(values), tuple(others)))[0]


def dot_width(rows, weights):
    return lax.dot_general(rows, weights, (((1,), (0,)), ((), ())), preferred_element_type=F32)


def dot_rows(left, right):
    return lax.dot_general(left, right, (((0,), (0,)), ((), ())), preferred_element_type=F32)


def call(kernel, out_shape, operands, scalars, work=4 * 10**9, unmoved=0, scratch=()):
    return pl.pallas_call(
        kernel,
        out_shape=out_shape,
        in_specs=[pl.BlockSpec(memory_space=pltpu.SMEM)]
        + [pl.BlockSpec(memory_space=pltpu.HBM)] * unmoved
        + [pl.BlockSpec(memory_space=pltpu.VMEM)] * (len(operands) - unmoved),
        out_specs=[pl.BlockSpec(memory_space=pltpu.VMEM)] * len(out_shape),
        scratch_shapes=list(scratch),
        compiler_params=pltpu.CompilerParams(vmem_limit_bytes=VMEM_LIMIT),
        cost_estimate=pl.CostEstimate(flops=work, bytes_accessed=0, transcendentals=0),
    )(scalars, *operands)


def picked(core, first, second):
    return jnp.where(core == 0, first, second)


def diagonal(count):
    across = lax.broadcasted_iota(jnp.int32, (count, count), 0)
    along = lax.broadcasted_iota(jnp.int32, (count, count), 1)
    return across == along


def column_of(row):
    return jnp.sum(jnp.where(diagonal(row.shape[1]), row, 0.0), axis=1, keepdims=True)


def row_of(column):
    return jnp.sum(jnp.where(diagonal(column.shape[0]), column, 0.0), axis=0, keepdims=True)


def pieces_of(value):
    high = value.astype(BF16).astype(F32)
    middle = (value - high).astype(BF16).astype(F32)
    return high, middle, value - high - middle


def prepare(core, local_ref, arrived_ref, flat_ref, mine_ref, other_ref):
    units, width = local_ref.shape[0], local_ref.shape[1] // 2
    at = pl.ds(pl.multiple_of(core * units, units), units)
    mine = pl.ds(pl.multiple_of(core * width, width), width)
    other = pl.ds(pl.multiple_of((1 - core) * width, width), width)
    block = local_ref[:, mine]
    flat_ref[at, :] = block
    mine_ref[:, at] = block.T
    other_ref[:, at] = local_ref[:, other].T
    came = pl.ds(pl.multiple_of((1 - core) * units, units), units)
    if arrived_ref.shape[1] > width:
        block, beside = arrived_ref[:, mine], arrived_ref[:, other]
    else:
        start = arrived_ref.shape[0] - 2 * units
        mine = pl.ds(pl.multiple_of(start + core * units, LANES), units)
        other = pl.ds(pl.multiple_of(start + (1 - core) * units, LANES), units)
        block, beside = arrived_ref[mine, :], arrived_ref[other, :]
    flat_ref[came, :] = block
    mine_ref[:, came] = block.T
    other_ref[:, came] = beside.T


def stacked(values):
    return jnp.concatenate(values, axis=0) if len(values) > 1 else values[0]


def give_next(core, refs):
    out_ref = refs[-1]
    half = out_ref.shape[0] // 2
    cut = refs[0].shape[0] - 2 * half
    out_ref[:half, :] = picked(core, refs[1][:half, :], refs[0][:half, :])
    out_ref[half:, :] = picked(core, refs[1][half + cut :, :], refs[0][half + cut :, :])
    return refs[2:-1]


def table_parts(expert, rows, width, experts):
    per_row = width // rows
    deep = -(-experts // per_row)
    line = lax.broadcasted_iota(jnp.int32, (EXTRA, width), 0)
    lane = lax.broadcasted_iota(jnp.int32, (EXTRA, width), 1)
    lanes = lane // rows == lax.rem(expert, per_row)
    return [lanes & (line == i * deep + expert // per_row) for i in range(3)]


def payload_kernel(experts, scalars, routes_hbm, gates_hbm, cotangent_hbm, out_ref, routes_ref, gates_ref, sems):
    rows, width = cotangent_hbm.shape
    half = rows // 2
    copies = [
        pltpu.make_async_copy(routes_hbm, routes_ref, sems.at[0]),
        pltpu.make_async_copy(gates_hbm, gates_ref, sems.at[1]),
        pltpu.make_async_copy(
            cotangent_hbm.at[pl.ds(0, half), :], out_ref.at[pl.ds(0, half), :], sems.at[2]
        ),
        pltpu.make_async_copy(
            cotangent_hbm.at[pl.ds(half, half), :],
            out_ref.at[pl.ds(half + EXTRA, half), :],
            sems.at[3],
        ),
    ]
    for copy in copies:
        copy.start()
    copies[0].wait()
    copies[1].wait()
    table = jnp.zeros((EXTRA, width), F32)
    for expert in range(experts):
        named = jnp.where(routes_ref[...] == expert, gates_ref[...], 0.0)
        row = jnp.sum(named, axis=0, keepdims=True)
        for piece, place in zip(pieces_of(row), table_parts(expert, rows, width, experts)):
            spread = jnp.concatenate([piece] * (width // rows), axis=1)
            table = jnp.where(place, spread, table)
    out_ref[half : half + EXTRA, :] = table.astype(BF16)
    copies[2].wait()
    copies[3].wait()


def gate_column(extra, expert, rows, experts):
    width = extra.shape[1]
    places = table_parts(expert, rows, width, experts)
    values = extra.astype(F32)
    row = sum(jnp.sum(jnp.where(p, values, 0.0), axis=0, keepdims=True) for p in places)
    row = sum(row[:, i * rows : (i + 1) * rows] for i in range(width // rows))
    return column_of(row)


def first_tokens_kernel(scalars, first, second, tokens, cotangent, out_ref):
    core = scalars[0]
    rows = first.shape[0]
    half = rows // 2
    out_ref[:rows, :] = picked(core, second[...], first[...])
    for i, ref in enumerate((tokens, cotangent)):
        at = rows + i * half
        out_ref[at : at + half, :] = picked(core, ref[half:rows, :], ref[:half, :])


def first_cotangent_kernel(scalars, first, second, w_ref, out_ref, sems):
    core = scalars[0]
    units, width = w_ref.shape[0], out_ref.shape[1]
    rows = out_ref.shape[0] - 2 * units
    half = rows // 2
    copies = [
        pltpu.make_async_copy(
            w_ref.at[:, pl.ds(i * width, width)],
            out_ref.at[pl.ds(rows + i * units, units), :],
            sems.at[i],
        )
        for i in range(2)
    ]
    for copy in copies:
        copy.start()
    out_ref[:half, :] = picked(core, second[:half, :], first[:half, :])
    out_ref[half:rows, :] = picked(core, second[half + EXTRA :, :], first[half + EXTRA :, :])
    for copy in copies:
        copy.wait()


def pick_kernel(scalars, first, second, out_ref):
    out_ref[...] = picked(scalars[0], second[...], first[...])


def taken(kinds, refs):
    pieces = []
    for kind in kinds:
        count = 2 if isinstance(kind, int) else 3
        pieces.append((kind, refs[:count]))
        refs = refs[count:]
    return pieces, refs


def rows_of(core, piece, rows):
    kind, refs = piece
    half = rows // 2
    if kind == "full":
        first, second, other = refs
        mine, there = picked(core, first[...], second[...]), other[...]
        if mine.shape[0] == rows:
            return mine, there, None
        extra = mine[half : half + EXTRA]
        mine = stacked([mine[:half], mine[half + EXTRA :]])
        if there.shape[0] > rows:
            there = stacked([there[:half], there[half + EXTRA :]])
        return mine, there, extra
    if kind == "far":
        first, second, other = refs
        if first.shape[0] == half:
            return picked(core, first[...], second[...]), other[...], None
        there = picked(core, other[:half, :], other[EXTRA:, :])
    else:
        block, arrived = refs
        there = arrived[kind : kind + half, :]
        if block.shape[0] == rows:
            return picked(core, block[:half, :], block[half:, :]), there, None
        first, second = block.at[: half + EXTRA, :], block.at[half:, :]
    mine = picked(core, first[:half, :], second[EXTRA:, :])
    return mine, there, picked(core, first[half:, :], second[:EXTRA, :])


def units_of(core, pieces, rows, w_ref, w_other_ref):
    here, there, extra = zip(*(rows_of(core, p, rows) for p in pieces))
    wide = dot_width(stacked(here), w_ref[...]) + dot_width(stacked(there), w_other_ref[...])
    return wide, extra


def forward_kernel(kinds, rows, with_next, with_weights, scalars, *refs):
    core = scalars[0]
    if with_weights:
        weights = refs[-2:]
        prepare(core, *refs[:2], *refs[-3:])
        refs = refs[2:-3]
    if with_next:
        refs = give_next(core, refs)
    hidden_ref, slope_ref = refs[-2:]
    pieces, refs = taken(kinds, refs)
    if not with_weights:
        weights = refs[:2]
    pre = units_of(core, pieces, rows, *weights)[0]
    logistic = 1.0 / (1.0 + jnp.exp(-pre))
    hidden_ref[...] = (pre * logistic).astype(BF16)
    slope_ref[...] = logistic * (1.0 + pre * (1.0 - logistic))


def backward_kernel(kinds, rows, experts, with_next, with_weights, before, scalars, *refs):
    core, expert = scalars[0], scalars[1]
    if with_weights:
        weights = refs[-2:]
        prepare(core, *refs[:2], *refs[-3:])
        refs = refs[2:-3]
    if with_next:
        refs = give_next(core, refs)
    if before:
        lines = refs[0].shape[0]
        for i in range(before):
            refs[-1][i * lines : (i + 1) * lines, :] = refs[i][...]
        refs = (*refs[before:-1], refs[-1].at[before * lines :, :])
    hidden_ref, slope_ref, out_ref = refs[-3:]
    pieces, refs = taken(kinds, refs)
    if not with_weights:
        weights = refs[:2]
    lines, units = hidden_ref.shape
    wide, extras = units_of(core, pieces, rows, *weights)
    columns = []
    for extra in extras:
        column = gate_column(extra, expert, rows, experts)
        if len(kinds) > 1:
            column = picked(core, column[: rows // 2], column[rows // 2 :])
        columns.append(column)
    gate = stacked(columns)
    hidden = hidden_ref[...].astype(F32)
    out_ref[:, :units] = (gate * hidden).astype(BF16)
    out_ref[:, units : 2 * units] = (gate * slope_ref[...] * wide).astype(BF16)
    sums = jnp.sum(hidden * wide, axis=1, keepdims=True)
    lane = lax.broadcasted_iota(jnp.int32, (lines, LANES), 1)
    kept = jnp.zeros((lines, LANES), F32)
    for i, piece in enumerate(pieces_of(sums)):
        kept = jnp.where(lane == i, piece, kept)
    out_ref[:, 2 * units : 2 * units + LANES] = kept.astype(BF16)


def dots_rows(expert, dots, start, rows, width, experts):
    count = dots.shape[0]
    row = row_of(dots)
    if count < rows:
        blank = jnp.zeros((1, count), F32)
        row = jnp.concatenate([row, blank] if start == 0 else [blank, row], axis=1)
    out = jnp.zeros((EXTRA, width), F32)
    for piece, place in zip(pieces_of(row), table_parts(expert, rows, width, experts)):
        out = jnp.where(place, jnp.concatenate([piece] * (width // rows), axis=1), out)
    return out


def return_kernel(kind, at, first_row, count, experts, rows, scalars, mine_ref, arrived_ref, w_ref, *refs):
    core, expert = scalars[0], scalars[1]
    units, width = w_ref.shape
    if kind == "far":
        lanes = slice(at, at + units + (LANES if at else 0))
        mine_all = mine_ref[first_row : first_row + count, lanes]
        arrived_all = arrived_ref[first_row : first_row + count, lanes]
    else:
        mine_here, arrived_here, w_here, sems = refs[-4:]
        refs = refs[:-4]
        window = (pl.ds(first_row, count), pl.ds(at, mine_here.shape[1]))
        copies = [
            pltpu.make_async_copy(mine_ref.at[window], mine_here, sems.at[0]),
            pltpu.make_async_copy(arrived_ref.at[window], arrived_here, sems.at[1]),
            pltpu.make_async_copy(w_ref, w_here, sems.at[2]),
        ]
        for copy in copies:
            copy.start()
        for copy in copies:
            copy.wait()
        mine_all, arrived_all, w_ref = mine_here[...], arrived_here[...], w_here
    mine, arrived = mine_all[:, :units], arrived_all[:, :units]
    both = jnp.concatenate([picked(core, mine, arrived), picked(core, arrived, mine)], axis=0)
    part = dot_width(both, w_ref[...])
    with_dots = at > 0
    extra = [None, None]
    if with_dots:
        mine = jnp.sum(mine_all[:, units:].astype(F32), axis=1, keepdims=True)
        arrived = jnp.sum(arrived_all[:, units:].astype(F32), axis=1, keepdims=True)
        dots = [picked(core, mine, arrived), picked(core, arrived, mine)]
        starts = (0, count if count < rows else 0)
        extra = [
            dots_rows(expert, d, start, rows, width, experts) for d, start in zip(dots, starts)
        ]
    if kind == "far":
        for i, out_ref in enumerate(refs):
            out_ref[:count, :] = part[i * count : (i + 1) * count].astype(BF16)
            if with_dots:
                out_ref[count:, :] = extra[i].astype(BF16)
        return
    from_ahead, from_behind = refs[:2]
    if kind == "own":
        total = part + from_ahead[:rows, :].astype(F32) + from_behind[:rows, :].astype(F32)
        if not with_dots:
            refs[2][...] = total.astype(BF16)
            return
        routes_ref, out_ref, gates_ref = refs[2:]
        out_ref[...] = total.astype(BF16)
        table = extra[0] + extra[1]
        table = table + from_ahead[rows:, :].astype(F32) + from_behind[rows:, :].astype(F32)
        per_row = width // rows
        deep = -(-experts // per_row)
        routes = routes_ref[...]
        grads = jnp.zeros(routes.shape, F32)
        for e in range(experts):
            lanes = slice((e % per_row) * rows, (e % per_row + 1) * rows)
            line = e // per_row
            row = sum(table[i * deep + line : i * deep + line + 1, lanes] for i in range(3))
            grads = jnp.where(routes == e, row, grads)
        gates_ref[...] = grads
        return
    behind_ref, ahead_ref = refs[2:]
    behind, ahead = part[:count], part[count:]
    if kind == "join":
        half = count // 2
        behind_ref[:half, :] = (behind[:half] + from_ahead[:half, :].astype(F32)).astype(BF16)
        behind_ref[half:count, :] = behind[half:].astype(BF16)
        ahead_ref[:half, :] = ahead[:half].astype(BF16)
        ahead_ref[half:count, :] = (ahead[half:] + from_behind[:half, :].astype(F32)).astype(BF16)
    else:
        half = count
        behind_ref[:count, :] = (behind + from_ahead[:count, :].astype(F32)).astype(BF16)
        ahead_ref[:count, :] = (ahead + from_behind[:count, :].astype(F32)).astype(BF16)
    if with_dots:
        behind_ref[count:, :] = (extra[0] + from_ahead[half:, :].astype(F32)).astype(BF16)
        ahead_ref[count:, :] = (extra[1] + from_behind[half:, :].astype(F32)).astype(BF16)


def weight_kernel(at, rows, scalars, *refs):
    core = scalars[0]
    lefts = []
    mine_ref, other_ref = refs[-2:]
    taken = 0
    if at:
        taken = 2
        units = refs[0].shape[0]
        mine_ref[:units, :] = refs[0][...]
        other_ref[:units, :] = refs[1][...]
        mine_ref, other_ref = mine_ref.at[units:, :], other_ref.at[units:, :]
    units = mine_ref.shape[0]
    above, above_came, ends, ends_came = refs[taken : taken + 4]
    rights = refs[taken + 4 : -2]
    for left, came in ((above, above_came), (ends, ends_came)):
        count = ends.shape[0]
        for i in range(left.shape[0] // count):
            lines = slice(i * count, (i + 1) * count)
            here, there = left[lines, at : at + 2 * units], came[lines, at : at + 2 * units]
            lefts += [picked(core, here, there), picked(core, there, here)]
    half = rows // 2
    block, far_first, far_second = rights[-3:]
    cut = block.shape[0] - rows
    blocks = []
    for ref in rights[:-3]:
        blocks += [ref[:half, :], ref[half + cut :, :]] if cut else [ref[...]]
    blocks += [block[:half, :], far_first[:half, :]]
    blocks += [block[half + cut :, :], far_second[cut:, :]]
    part = dot_rows(stacked(lefts), stacked(blocks))
    mine_ref[...] = picked(core, part[:units], part[units:]).astype(BF16)
    other_ref[...] = picked(core, part[units:], part[:units]).astype(BF16)


def send_kernel(scalars, mine_ref, came_ref, sent_ref, kept_ref):
    @pl.when(scalars[2] == 0)
    def _():
        sent_ref[...] = came_ref[...]
        kept_ref[...] = mine_ref[...]

    @pl.when(scalars[2] != 0)
    def _():
        sent_ref[...] = mine_ref[...]
        kept_ref[...] = came_ref[...]


def add_kernel(*refs):
    for i in range(2):
        refs[4 + i][...] = refs[2 * i][...].astype(F32) + refs[2 * i + 1][...].astype(F32)


def per_device(tokens, routes, gates, w_in, w_out, cotangent):
    size = lax.axis_size("expert")
    n_dp = lax.axis_size("dp")
    rows, width = tokens.shape
    half = rows // 2
    experts = size * w_in.shape[0]
    core = lax.axis_index("tensor")
    place = lax.axis_index("expert")
    group = lax.axis_index("dp")
    order = ring_order(size)
    onward_pairs = [(order[i], order[(i + 1) % size]) for i in range(size)]
    back_pairs = [(b, a) for a, b in onward_pairs]
    steps = size // 2
    w_in, w_out = w_in[0], w_out[0]
    local_units = w_in.shape[0]
    units = 2 * local_units

    def both_ways(forth_value, back_value, name):
        with jax.named_scope("onward_" + name):
            forth = lax.ppermute(forth_value, "expert", onward_pairs)
        with jax.named_scope("back_" + name):
            return forth, lax.ppermute(back_value, "expert", back_pairs)

    scalars = jnp.stack([core, place, (core + group) % 2]).astype(jnp.int32)

    weight_shapes = [
        jax.ShapeDtypeStruct((units, width), BF16),
        jax.ShapeDtypeStruct((width, units), BF16),
        jax.ShapeDtypeStruct((width, units), BF16),
    ]

    def split(pieces):
        return tuple(p[0] for p in pieces), [v for p in pieces for v in p[1:]]

    def forward(pieces, weights, following=()):
        shape = (rows, units)
        raw = weights[0] is w_in
        kinds, operands = split(pieces)
        result = call(
            functools.partial(forward_kernel, kinds, rows, len(following) > 0, raw),
            [
                jax.ShapeDtypeStruct(shape, BF16),
                jax.ShapeDtypeStruct(shape, F32),
                *[jax.ShapeDtypeStruct((rows, width), BF16) for _ in following[:1]],
                *(weight_shapes if raw else ()),
            ],
            [
                *(weights if raw else ()),
                *following,
                *operands,
                *(() if raw else weights[1:]),
            ],
            scalars,
        )
        return (result[:-3], result[-3:]) if raw else (result, weights)

    def backward(pieces, weights, hidden, slope, following=(), before=()):
        count = hidden.shape[0] * (1 + len(before))
        raw = weights[0] is w_out
        kinds, operands = split(pieces)
        result = call(
            functools.partial(
                backward_kernel, kinds, rows, experts, len(following) > 0, raw, len(before)
            ),
            [
                jax.ShapeDtypeStruct((count, 2 * units + LANES), BF16),
                *[jax.ShapeDtypeStruct((rows, width), BF16) for _ in following[:1]],
                *(weight_shapes if raw else ()),
            ],
            [
                *(weights if raw else ()),
                *following,
                *before,
                *operands,
                *(() if raw else weights[1:]),
                hidden,
                slope,
            ],
            scalars,
        )
        return (result[:-3], result[-3:]) if raw else (result, weights)

    def returned(kind, at, first_row, mine, arrived, weights, sums, more=()):
        count = rows if kind in ("join", "add") else half
        extra = EXTRA if at else 0
        if kind == "own":
            shapes = [jax.ShapeDtypeStruct((rows, width), BF16)]
            if at:
                shapes.append(jax.ShapeDtypeStruct(routes.shape[::-1], F32))
        else:
            shapes = [jax.ShapeDtypeStruct((count + extra, width), BF16)] * 2
        kernel = functools.partial(return_kernel, kind, at, first_row, count, experts, rows)
        operands = [mine, arrived, weights, *sums, *more]
        if kind == "far":
            return call(kernel, shapes, operands, scalars, 3 * 10**9)
        held = (count, units + (LANES if at else 0))
        scratch = [
            pltpu.VMEM(held, BF16),
            pltpu.VMEM(held, BF16),
            pltpu.VMEM((units, width), BF16),
            pltpu.SemaphoreType.DMA((3,)),
        ]
        return call(kernel, shapes, operands, scalars, 2 * 10**9, 3, scratch)

    payload = pl.pallas_call(
        functools.partial(payload_kernel, experts),
        out_shape=jax.ShapeDtypeStruct((rows + EXTRA, width), BF16),
        in_specs=[pl.BlockSpec(memory_space=pltpu.SMEM)]
        + [pl.BlockSpec(memory_space=pltpu.HBM)] * 3,
        out_specs=pl.BlockSpec(memory_space=pltpu.VMEM),
        scratch_shapes=[
            pltpu.VMEM(routes.shape[::-1], jnp.int32),
            pltpu.VMEM(gates.shape[::-1], F32),
            pltpu.SemaphoreType.DMA((4,)),
        ],
        compiler_params=pltpu.CompilerParams(vmem_limit_bytes=VMEM_LIMIT),
        cost_estimate=pl.CostEstimate(flops=10**9, bytes_accessed=0, transcendentals=0),
    )(scalars, routes.T, gates.T, cotangent)
    ring = [both_ways(tokens, tokens, "tok1"), both_ways(payload, payload, "cot1")]

    in_all, out_all = (w_in, swap_cores(w_in, "weights")), ()

    arrivals, outputs, lefts = [], [], []
    for turn in range(2 * steps):
        now = ring[turn]
        step = turn // 2 + 1
        name = ("tok", "cot")[turn % 2]
        sent = None
        if turn == 0:
            sent = call(
                first_tokens_kernel,
                [jax.ShapeDtypeStruct((2 * rows, width), BF16)],
                [*now, tokens, cotangent],
                scalars,
                2 * 10**9,
            )[0]
        elif turn == 1:
            seen = tied((*now, w_out), (*in_all, sent_first))
            cot_sent = pl.pallas_call(
                first_cotangent_kernel,
                out_shape=jax.ShapeDtypeStruct((rows + units, width), BF16),
                in_specs=[pl.BlockSpec(memory_space=pltpu.SMEM)]
                + [pl.BlockSpec(memory_space=pltpu.VMEM)] * 2
                + [pl.BlockSpec(memory_space=pltpu.HBM)],
                out_specs=pl.BlockSpec(memory_space=pltpu.VMEM),
                scratch_shapes=[pltpu.SemaphoreType.DMA((2,))],
                compiler_params=pltpu.CompilerParams(vmem_limit_bytes=VMEM_LIMIT),
                cost_estimate=pl.CostEstimate(flops=10**9, bytes_accessed=0, transcendentals=0),
            )(scalars, *seen)
            result, in_all = forward([("full", *arrivals[0])], in_all)
            outputs.append(result)
        elif turn < 2 * steps - 1:
            done = turn - 1
            first, second, other = arrivals[done]
            following = now if turn < 2 * steps - 3 else ()
            if turn == 2 * steps - 3:
                other = tied((other,), now)[0]
            pieces = [("full", first, second, other)]
            if done % 2 == 0:
                result, in_all = forward(pieces, in_all, following)
                if following:
                    *result, sent = result
                outputs.append(result)
            else:
                before = lefts if turn == 2 * steps - 2 else ()
                result, out_all = backward(
                    pieces, out_all, *outputs[done - 1], following, before
                )
                if following:
                    *result, sent = result
                lefts.append(result[0])
                outputs.append(result)
            if turn != 2 * steps - 3:
                now = tied(now, outputs[-1][:1])
        else:
            now = tied(now, outputs[-1])
        if turn == 0:
            sent_first = sent
        elif turn == 1:
            sent = cot_sent
        elif sent is None:
            shape = [jax.ShapeDtypeStruct(now[0].shape, BF16)]
            sent = call(pick_kernel, shape, [*now], scalars, 10**8)[0]
        if step < steps - 1:
            ring.append(both_ways(now[0], now[1], name + str(step + 1)))
        elif step == steps - 1:
            cut = half + (EXTRA if turn % 2 else 0)
            ends = ring[turn][0][:cut], ring[turn][1][half:]
            ring.append(both_ways(*ends, name + str(step + 1)))
        other = swap_cores(sent, name + str(step))
        if turn == 0:
            own_arrived, other = other, other[:rows]
        elif turn == 1:
            out_all, other = (w_out, other), other[:rows]
        arrivals.append((*now, other))
    tok_pieces = [(rows, tokens, own_arrived), ("far", *arrivals[2 * steps - 2])]
    cot_pieces = [(rows + half, payload, own_arrived), ("far", *arrivals[2 * steps - 1])]
    lefts = lefts[-1]
    lefts_arrived = swap_cores(lefts, "lefts")
    hidden, slope = forward(tok_pieces, in_all)[0]
    ends = backward(cot_pieces, out_all, hidden, slope)[0][0]
    ends_arrived = swap_cores(ends, "ends")

    sent = returned("far", 0, half, ends, ends_arrived, out_all[0], ())
    mixed_in = both_ways(sent[1], sent[0], "mixed")[::-1]
    ends_after = tied((ends_arrived,), sent)[0]
    sent = returned("far", units, half, ends, ends_after, in_all[0], ())
    back_in = both_ways(sent[1], sent[0], "grad")[::-1]

    def weight_part(at, which, after, above):
        operands = [*above, lefts, lefts_arrived, ends, tied((ends_arrived,), after)[0]]
        for s in range(steps - 1):
            operands += arrivals[2 * s + which][:2]
        own, far_ends = (tok_pieces, cot_pieces)[which]
        operands += [own[1], *far_ends[1:3]]
        deep = local_units * (1 + len(above) // 2)
        return call(
            functools.partial(weight_kernel, at, rows),
            [jax.ShapeDtypeStruct((deep, width), BF16)] * 2,
            operands,
            scalars,
            2 * 10**9,
        )

    part_out = weight_part(0, 1, sent, ())
    parts, parts_other = weight_part(units, 0, (*part_out, *mixed_in, *back_in), part_out)
    parts_other = swap_cores(parts_other, "grad")
    for step in range(steps - 1, 0, -1):
        kind = "join" if step == steps - 1 else "add"
        line = (step - 1) * rows
        mixed_in = tied(mixed_in, (*sent, *((parts,) if kind == "join" else ())))
        sent = returned(kind, 0, line, lefts, lefts_arrived, out_all[0], mixed_in)
        mixed_in = both_ways(sent[1], sent[0], "mixed")[::-1]
        back_in = tied(back_in, sent)
        sent = returned(kind, units, line, lefts, lefts_arrived, in_all[0], back_in)
        back_in = both_ways(sent[1], sent[0], "grad")[::-1]
        if kind == "join":
            parts_other = tied((parts_other,), sent)[0]
            if n_dp == 2:
                tile = units // 4
                block = pl.BlockSpec((tile, width), lambda i: (i, 0))
                parts_sent, parts_kept = pl.pallas_call(
                    send_kernel,
                    grid=(4,),
                    out_shape=[jax.ShapeDtypeStruct(parts.shape, BF16)] * 2,
                    in_specs=[pl.BlockSpec(memory_space=pltpu.SMEM), block, block],
                    out_specs=[block] * 2,
                    compiler_params=pltpu.CompilerParams(vmem_limit_bytes=VMEM_LIMIT),
                    cost_estimate=pl.CostEstimate(flops=10**9, bytes_accessed=0, transcendentals=0),
                )(scalars, parts, parts_other)
                parts_came = lax.ppermute(parts_sent, "dp", [(0, 1), (1, 0)])
            else:
                totals = []
                for i in range(2):
                    piece = slice(i * local_units, (i + 1) * local_units)
                    mine, arrived = parts[piece], parts_other[piece]
                    part = jnp.concatenate(
                        [picked(core, mine, arrived), picked(core, arrived, mine)], axis=1
                    )
                    across = part.shape[1] // n_dp
                    slices = [
                        lax.dynamic_slice_in_dim(part, ((group + shift) % n_dp) * across, across, axis=1)
                        for shift in range(n_dp)
                    ]
                    total = slices[0].astype(F32)
                    for shift in range(1, n_dp):
                        pairs = [(i, (i + shift) % n_dp) for i in range(n_dp)]
                        total = total + lax.ppermute(slices[shift], "dp", pairs).astype(F32)
                    totals.append(total)
            if n_dp == 2:
                sent = (*sent, parts_sent)
    mixed_in = tied(mixed_in, sent)
    if n_dp == 2:
        tiles = 3 if local_units % 48 == 0 else 1
        block = (local_units // tiles, width)
        upper = pl.BlockSpec(block, lambda i: (i, 0))
        lower = pl.BlockSpec(block, lambda i: (i + tiles, 0))
        totals = pl.pallas_call(
            add_kernel,
            grid=(tiles,),
            out_shape=[jax.ShapeDtypeStruct((local_units, width), F32)] * 2,
            in_specs=[upper] * 2 + [lower] * 2,
            out_specs=[upper] * 2,
            compiler_params=pltpu.CompilerParams(vmem_limit_bytes=VMEM_LIMIT),
            cost_estimate=pl.CostEstimate(flops=10**9, bytes_accessed=0, transcendentals=0),
        )(*([parts_kept, parts_came] * 2))
    back_in = tied(back_in, totals)
    mixed = returned("own", 0, 0, ends, ends_arrived, out_all[0], mixed_in)[0]
    grad_tokens, grad_gates = returned(
        "own", units, 0, ends, ends_arrived, in_all[0], back_in, (routes.T,)
    )
    grad_gates = grad_gates.T

    grad_out, grad_in = totals
    return (mixed, grad_tokens, grad_gates, grad_in[None], grad_out[None])


def solution(mesh):
    placed = (
        P(("dp", "expert"), "tensor"),
        P(("dp", "expert"), None),
        P(("dp", "expert"), None),
        P("expert", "tensor", None),
        P("expert", "tensor", None),
        P(("dp", "expert"), "tensor"),
    )
    return jax.shard_map(
        per_device,
        mesh=mesh,
        in_specs=placed,
        out_specs=(
            P(("dp", "expert"), "tensor"),
            P(("dp", "expert"), "tensor"),
            P(("dp", "expert"), None),
            P("expert", "tensor", "dp"),
            P("expert", "tensor", "dp"),
        ),
        check_vma=False,
    )
```

```python
import functools

import jax
import jax.numpy as jnp
from jax import lax
from jax.experimental import pallas as pl
from jax.experimental.pallas import tpu as pltpu
from jax.sharding import PartitionSpec as P

BF16 = jnp.bfloat16
F32 = jnp.float32
VMEM_LIMIT = 16 * 1024 * 1024
LANES = 128
EXTRA = 16


def ring_order(count):
    if count % 2:
        return list(range(count))
    return list(range(0, count, 2)) + list(range(count - 1, 0, -2))


def swap_cores(value, name):
    with jax.named_scope("swap_" + name):
        return lax.ppermute(value, "tensor", [(0, 1), (1, 0)])


def tied(values, others):
    return lax.optimization_barrier((tuple(values), tuple(others)))[0]


def dot_width(rows, weights):
    return lax.dot_general(rows, weights, (((1,), (0,)), ((), ())), preferred_element_type=F32)


def dot_rows(left, right):
    return lax.dot_general(left, right, (((0,), (0,)), ((), ())), preferred_element_type=F32)


def call(kernel, out_shape, operands, scalars, work=4 * 10**9):
    return pl.pallas_call(
        kernel,
        out_shape=out_shape,
        in_specs=[pl.BlockSpec(memory_space=pltpu.SMEM)]
        + [pl.BlockSpec(memory_space=pltpu.VMEM)] * len(operands),
        out_specs=[pl.BlockSpec(memory_space=pltpu.VMEM)] * len(out_shape),
        compiler_params=pltpu.CompilerParams(vmem_limit_bytes=VMEM_LIMIT),
        cost_estimate=pl.CostEstimate(flops=work, bytes_accessed=0, transcendentals=0),
    )(scalars, *operands)


def picked(core, first, second):
    return jnp.where(core == 0, first, second)


def diagonal(count):
    across = lax.broadcasted_iota(jnp.int32, (count, count), 0)
    along = lax.broadcasted_iota(jnp.int32, (count, count), 1)
    return across == along


def column_of(row):
    return jnp.sum(jnp.where(diagonal(row.shape[1]), row, 0.0), axis=1, keepdims=True)


def row_of(column):
    return jnp.sum(jnp.where(diagonal(column.shape[0]), column, 0.0), axis=0, keepdims=True)


def pieces_of(value):
    high = value.astype(BF16).astype(F32)
    middle = (value - high).astype(BF16).astype(F32)
    return high, middle, value - high - middle


def prepare(core, local_ref, arrived_ref, flat_ref, mine_ref, other_ref):
    units, width = local_ref.shape[0], local_ref.shape[1] // 2
    at = pl.ds(pl.multiple_of(core * units, units), units)
    mine = pl.ds(pl.multiple_of(core * width, width), width)
    other = pl.ds(pl.multiple_of((1 - core) * width, width), width)
    block = local_ref[:, mine]
    flat_ref[at, :] = block
    mine_ref[:, at] = block.T
    other_ref[:, at] = local_ref[:, other].T
    came = pl.ds(pl.multiple_of((1 - core) * units, units), units)
    if arrived_ref.shape[1] > width:
        block, beside = arrived_ref[:, mine], arrived_ref[:, other]
    else:
        start = arrived_ref.shape[0] - 2 * units
        mine = pl.ds(pl.multiple_of(start + core * units, LANES), units)
        other = pl.ds(pl.multiple_of(start + (1 - core) * units, LANES), units)
        block, beside = arrived_ref[mine, :], arrived_ref[other, :]
    flat_ref[came, :] = block
    mine_ref[:, came] = block.T
    other_ref[:, came] = beside.T


def stacked(values):
    return jnp.concatenate(values, axis=0) if len(values) > 1 else values[0]


def give_next(core, refs):
    out_ref = refs[-1]
    half = out_ref.shape[0] // 2
    cut = refs[0].shape[0] - 2 * half
    out_ref[:half, :] = picked(core, refs[1][:half, :], refs[0][:half, :])
    out_ref[half:, :] = picked(core, refs[1][half + cut :, :], refs[0][half + cut :, :])
    return refs[2:-1]


def table_parts(expert, rows, width, experts):
    per_row = width // rows
    deep = -(-experts // per_row)
    line = lax.broadcasted_iota(jnp.int32, (EXTRA, width), 0)
    lane = lax.broadcasted_iota(jnp.int32, (EXTRA, width), 1)
    lanes = lane // rows == lax.rem(expert, per_row)
    return [lanes & (line == i * deep + expert // per_row) for i in range(3)]


def payload_kernel(experts, routes_hbm, gates_hbm, cotangent_hbm, out_ref, routes_ref, gates_ref, sems):
    rows, width = cotangent_hbm.shape
    half = rows // 2
    copies = [
        pltpu.make_async_copy(routes_hbm, routes_ref, sems.at[0]),
        pltpu.make_async_copy(gates_hbm, gates_ref, sems.at[1]),
        pltpu.make_async_copy(
            cotangent_hbm.at[pl.ds(0, half), :], out_ref.at[pl.ds(0, half), :], sems.at[2]
        ),
        pltpu.make_async_copy(
            cotangent_hbm.at[pl.ds(half, half), :],
            out_ref.at[pl.ds(half + EXTRA, half), :],
            sems.at[3],
        ),
    ]
    for copy in copies:
        copy.start()
    copies[0].wait()
    copies[1].wait()
    table = jnp.zeros((EXTRA, width), F32)
    for expert in range(experts):
        named = jnp.where(routes_ref[...] == expert, gates_ref[...], 0.0)
        row = jnp.sum(named, axis=0, keepdims=True)
        for piece, place in zip(pieces_of(row), table_parts(expert, rows, width, experts)):
            spread = jnp.concatenate([piece] * (width // rows), axis=1)
            table = jnp.where(place, spread, table)
    out_ref[half : half + EXTRA, :] = table.astype(BF16)
    copies[2].wait()
    copies[3].wait()


def gate_column(extra, expert, rows, experts):
    width = extra.shape[1]
    places = table_parts(expert, rows, width, experts)
    values = extra.astype(F32)
    row = sum(jnp.sum(jnp.where(p, values, 0.0), axis=0, keepdims=True) for p in places)
    row = sum(row[:, i * rows : (i + 1) * rows] for i in range(width // rows))
    return column_of(row)


def first_tokens_kernel(scalars, first, second, tokens, cotangent, out_ref):
    core = scalars[0]
    rows = first.shape[0]
    half = rows // 2
    out_ref[:rows, :] = picked(core, second[...], first[...])
    for i, ref in enumerate((tokens, cotangent)):
        at = rows + i * half
        out_ref[at : at + half, :] = picked(core, ref[half:rows, :], ref[:half, :])


def first_cotangent_kernel(scalars, first, second, w_ref, out_ref, sems):
    core = scalars[0]
    units, width = w_ref.shape[0], out_ref.shape[1]
    rows = out_ref.shape[0] - 2 * units
    half = rows // 2
    copies = [
        pltpu.make_async_copy(
            w_ref.at[:, pl.ds(i * width, width)],
            out_ref.at[pl.ds(rows + i * units, units), :],
            sems.at[i],
        )
        for i in range(2)
    ]
    for copy in copies:
        copy.start()
    out_ref[:half, :] = picked(core, second[:half, :], first[:half, :])
    out_ref[half:rows, :] = picked(core, second[half + EXTRA :, :], first[half + EXTRA :, :])
    for copy in copies:
        copy.wait()


def taken(kinds, refs):
    pieces = []
    for kind in kinds:
        count = 2 if isinstance(kind, int) else 3
        pieces.append((kind, refs[:count]))
        refs = refs[count:]
    return pieces, refs


def rows_of(core, piece, rows):
    kind, refs = piece
    half = rows // 2
    if kind == "full":
        first, second, other = refs
        mine, there = picked(core, first[...], second[...]), other[...]
        if mine.shape[0] == rows:
            return mine, there, None
        extra = mine[half : half + EXTRA]
        mine = stacked([mine[:half], mine[half + EXTRA :]])
        if there.shape[0] > rows:
            there = stacked([there[:half], there[half + EXTRA :]])
        return mine, there, extra
    if kind == "far":
        first, second, other = refs
        if first.shape[0] == half:
            return picked(core, first[...], second[...]), other[...], None
        there = picked(core, other[:half, :], other[EXTRA:, :])
    else:
        block, arrived = refs
        there = arrived[kind : kind + half, :]
        if block.shape[0] == rows:
            return picked(core, block[:half, :], block[half:, :]), there, None
        first, second = block.at[: half + EXTRA, :], block.at[half:, :]
    mine = picked(core, first[:half, :], second[EXTRA:, :])
    return mine, there, picked(core, first[half:, :], second[:EXTRA, :])


def units_of(core, pieces, rows, w_ref, w_other_ref):
    here, there, extra = zip(*(rows_of(core, p, rows) for p in pieces))
    wide = dot_width(stacked(here), w_ref[...]) + dot_width(stacked(there), w_other_ref[...])
    return wide, extra


def forward_kernel(kinds, rows, with_next, with_weights, scalars, *refs):
    core = scalars[0]
    if with_weights:
        weights = refs[-2:]
        prepare(core, *refs[:2], *refs[-3:])
        refs = refs[2:-3]
    if with_next:
        refs = give_next(core, refs)
    hidden_ref, slope_ref = refs[-2:]
    pieces, refs = taken(kinds, refs)
    if not with_weights:
        weights = refs[:2]
    pre = units_of(core, pieces, rows, *weights)[0]
    logistic = 1.0 / (1.0 + jnp.exp(-pre))
    hidden_ref[...] = (pre * logistic).astype(BF16)
    slope_ref[...] = logistic * (1.0 + pre * (1.0 - logistic))


def backward_kernel(kinds, rows, experts, with_next, with_weights, before, scalars, *refs):
    core, expert = scalars[0], scalars[1]
    if with_weights:
        weights = refs[-2:]
        prepare(core, *refs[:2], *refs[-3:])
        refs = refs[2:-3]
    if with_next:
        refs = give_next(core, refs)
    if before:
        lines = refs[0].shape[0]
        for i in range(before):
            refs[-1][i * lines : (i + 1) * lines, :] = refs[i][...]
        refs = (*refs[before:-1], refs[-1].at[before * lines :, :])
    hidden_ref, slope_ref, out_ref = refs[-3:]
    pieces, refs = taken(kinds, refs)
    if not with_weights:
        weights = refs[:2]
    lines, units = hidden_ref.shape
    wide, extras = units_of(core, pieces, rows, *weights)
    columns = []
    for extra in extras:
        column = gate_column(extra, expert, rows, experts)
        if len(kinds) > 1:
            column = picked(core, column[: rows // 2], column[rows // 2 :])
        columns.append(column)
    gate = stacked(columns)
    hidden = hidden_ref[...].astype(F32)
    out_ref[:, :units] = (gate * hidden).astype(BF16)
    out_ref[:, units : 2 * units] = (gate * slope_ref[...] * wide).astype(BF16)
    sums = jnp.sum(hidden * wide, axis=1, keepdims=True)
    lane = lax.broadcasted_iota(jnp.int32, (lines, LANES), 1)
    kept = jnp.zeros((lines, LANES), F32)
    for i, piece in enumerate(pieces_of(sums)):
        kept = jnp.where(lane == i, piece, kept)
    out_ref[:, 2 * units : 2 * units + LANES] = kept.astype(BF16)


def dots_rows(expert, dots, start, rows, width, experts):
    count = dots.shape[0]
    row = row_of(dots)
    if count < rows:
        blank = jnp.zeros((1, count), F32)
        row = jnp.concatenate([row, blank] if start == 0 else [blank, row], axis=1)
    out = jnp.zeros((EXTRA, width), F32)
    for piece, place in zip(pieces_of(row), table_parts(expert, rows, width, experts)):
        out = jnp.where(place, jnp.concatenate([piece] * (width // rows), axis=1), out)
    return out


def return_kernel(kind, at, first_row, count, experts, rows, scalars, mine_ref, arrived_ref, w_ref, *refs):
    core, expert = scalars[0], scalars[1]
    units, width = w_ref.shape
    lanes = slice(at, at + units + (LANES if at else 0))
    mine_all = mine_ref[first_row : first_row + count, lanes]
    arrived_all = arrived_ref[first_row : first_row + count, lanes]
    mine, arrived = mine_all[:, :units], arrived_all[:, :units]
    both = jnp.concatenate([picked(core, mine, arrived), picked(core, arrived, mine)], axis=0)
    part = dot_width(both, w_ref[...])
    with_dots = at > 0
    extra = [None, None]
    if with_dots:
        mine = jnp.sum(mine_all[:, units:].astype(F32), axis=1, keepdims=True)
        arrived = jnp.sum(arrived_all[:, units:].astype(F32), axis=1, keepdims=True)
        dots = [picked(core, mine, arrived), picked(core, arrived, mine)]
        starts = (0, count if count < rows else 0)
        extra = [
            dots_rows(expert, d, start, rows, width, experts) for d, start in zip(dots, starts)
        ]
    if kind == "far":
        for i, out_ref in enumerate(refs):
            out_ref[:count, :] = part[i * count : (i + 1) * count].astype(BF16)
            if with_dots:
                out_ref[count:, :] = extra[i].astype(BF16)
        return
    from_ahead, from_behind = refs[:2]
    if kind == "own":
        total = part + from_ahead[:rows, :].astype(F32) + from_behind[:rows, :].astype(F32)
        if not with_dots:
            refs[2][...] = total.astype(BF16)
            return
        routes_ref, out_ref, gates_ref = refs[2:]
        out_ref[...] = total.astype(BF16)
        table = extra[0] + extra[1]
        table = table + from_ahead[rows:, :].astype(F32) + from_behind[rows:, :].astype(F32)
        per_row = width // rows
        deep = -(-experts // per_row)
        routes = routes_ref[...]
        grads = jnp.zeros(routes.shape, F32)
        for e in range(experts):
            lanes = slice((e % per_row) * rows, (e % per_row + 1) * rows)
            line = e // per_row
            row = sum(table[i * deep + line : i * deep + line + 1, lanes] for i in range(3))
            grads = jnp.where(routes == e, row, grads)
        gates_ref[...] = grads
        return
    behind_ref, ahead_ref = refs[2:]
    behind, ahead = part[:count], part[count:]
    if kind == "join":
        half = count // 2
        behind_ref[:half, :] = (behind[:half] + from_ahead[:half, :].astype(F32)).astype(BF16)
        behind_ref[half:count, :] = behind[half:].astype(BF16)
        ahead_ref[:half, :] = ahead[:half].astype(BF16)
        ahead_ref[half:count, :] = (ahead[half:] + from_behind[:half, :].astype(F32)).astype(BF16)
    else:
        half = count
        behind_ref[:count, :] = (behind + from_ahead[:count, :].astype(F32)).astype(BF16)
        ahead_ref[:count, :] = (ahead + from_behind[:count, :].astype(F32)).astype(BF16)
    if with_dots:
        behind_ref[count:, :] = (extra[0] + from_ahead[half:, :].astype(F32)).astype(BF16)
        ahead_ref[count:, :] = (extra[1] + from_behind[half:, :].astype(F32)).astype(BF16)


def weight_kernel(at, rows, scalars, *refs):
    core = scalars[0]
    lefts = []
    mine_ref, other_ref = refs[-2:]
    taken = 0
    if at:
        taken = 2
        units = refs[0].shape[0]
        mine_ref[:units, :] = refs[0][...]
        other_ref[:units, :] = refs[1][...]
        mine_ref, other_ref = mine_ref.at[units:, :], other_ref.at[units:, :]
    units = mine_ref.shape[0]
    above, above_came, ends, ends_came = refs[taken : taken + 4]
    rights = refs[taken + 4 : -2]
    for left, came in ((above, above_came), (ends, ends_came)):
        count = ends.shape[0]
        for i in range(left.shape[0] // count):
            lines = slice(i * count, (i + 1) * count)
            here, there = left[lines, at : at + 2 * units], came[lines, at : at + 2 * units]
            lefts += [picked(core, here, there), picked(core, there, here)]
    half = rows // 2
    block, far_first, far_second = rights[-3:]
    cut = block.shape[0] - rows
    blocks = []
    for ref in rights[:-3]:
        blocks += [ref[:half, :], ref[half + cut :, :]] if cut else [ref[...]]
    blocks += [block[:half, :], far_first[:half, :]]
    blocks += [block[half + cut :, :], far_second[cut:, :]]
    part = dot_rows(stacked(lefts), stacked(blocks))
    mine_ref[...] = picked(core, part[:units], part[units:]).astype(BF16)
    other_ref[...] = picked(core, part[units:], part[:units]).astype(BF16)


def send_kernel(scalars, mine_ref, came_ref, sent_ref, kept_ref):
    @pl.when(scalars[2] == 0)
    def _():
        sent_ref[...] = came_ref[...]
        kept_ref[...] = mine_ref[...]

    @pl.when(scalars[2] != 0)
    def _():
        sent_ref[...] = mine_ref[...]
        kept_ref[...] = came_ref[...]


def add_kernel(kept_ref, came_ref, first_hbm, second_hbm, held_ref, sems):
    tiles, rows = held_ref.shape[0], held_ref.shape[1]
    copies = []
    for i in range(tiles):
        at = slice(i * rows, (i + 1) * rows)
        held_ref[i] = kept_ref[at, :].astype(F32) + came_ref[at, :].astype(F32)
        out = first_hbm if i < tiles // 2 else second_hbm
        start = (i % (tiles // 2)) * rows
        copy = pltpu.make_async_copy(held_ref.at[i], out.at[pl.ds(start, rows), :], sems.at[i])
        copy.start()
        copies.append(copy)
    for copy in copies:
        copy.wait()


def per_device(tokens, routes, gates, w_in, w_out, cotangent):
    size = lax.axis_size("expert")
    n_dp = lax.axis_size("dp")
    rows, width = tokens.shape
    half = rows // 2
    experts = size * w_in.shape[0]
    core = lax.axis_index("tensor")
    place = lax.axis_index("expert")
    group = lax.axis_index("dp")
    order = ring_order(size)
    onward_pairs = [(order[i], order[(i + 1) % size]) for i in range(size)]
    back_pairs = [(b, a) for a, b in onward_pairs]
    steps = size // 2
    w_in, w_out = w_in[0], w_out[0]
    local_units = w_in.shape[0]
    units = 2 * local_units

    def both_ways(forth_value, back_value, name):
        with jax.named_scope("onward_" + name):
            forth = lax.ppermute(forth_value, "expert", onward_pairs)
        with jax.named_scope("back_" + name):
            return forth, lax.ppermute(back_value, "expert", back_pairs)

    first_core = lax.optimization_barrier(core == 0)
    core_now = jnp.where(first_core, 0, 1)
    scalars = jnp.stack([core_now, place, (core + group) % 2]).astype(jnp.int32)

    weight_shapes = [
        jax.ShapeDtypeStruct((units, width), BF16),
        jax.ShapeDtypeStruct((width, units), BF16),
        jax.ShapeDtypeStruct((width, units), BF16),
    ]

    def split(pieces):
        return tuple(p[0] for p in pieces), [v for p in pieces for v in p[1:]]

    def forward(pieces, weights, following=()):
        shape = (rows, units)
        raw = weights[0] is w_in
        kinds, operands = split(pieces)
        result = call(
            functools.partial(forward_kernel, kinds, rows, len(following) > 0, raw),
            [
                jax.ShapeDtypeStruct(shape, BF16),
                jax.ShapeDtypeStruct(shape, F32),
                *[jax.ShapeDtypeStruct((rows, width), BF16) for _ in following[:1]],
                *(weight_shapes if raw else ()),
            ],
            [
                *(weights if raw else ()),
                *following,
                *operands,
                *(() if raw else weights[1:]),
            ],
            scalars,
        )
        return (result[:-3], result[-3:]) if raw else (result, weights)

    def backward(pieces, weights, hidden, slope, following=(), before=()):
        count = hidden.shape[0] * (1 + len(before))
        raw = weights[0] is w_out
        kinds, operands = split(pieces)
        result = call(
            functools.partial(
                backward_kernel, kinds, rows, experts, len(following) > 0, raw, len(before)
            ),
            [
                jax.ShapeDtypeStruct((count, 2 * units + LANES), BF16),
                *[jax.ShapeDtypeStruct((rows, width), BF16) for _ in following[:1]],
                *(weight_shapes if raw else ()),
            ],
            [
                *(weights if raw else ()),
                *following,
                *before,
                *operands,
                *(() if raw else weights[1:]),
                hidden,
                slope,
            ],
            scalars,
        )
        return (result[:-3], result[-3:]) if raw else (result, weights)

    def returned(kind, at, first_row, mine, arrived, weights, sums, more=()):
        count = rows if kind in ("join", "add") else half
        extra = EXTRA if at else 0
        if kind == "own":
            shapes = [jax.ShapeDtypeStruct((rows, width), BF16)]
            if at:
                shapes.append(jax.ShapeDtypeStruct(routes.shape[::-1], F32))
        else:
            shapes = [jax.ShapeDtypeStruct((count + extra, width), BF16)] * 2
        kernel = functools.partial(return_kernel, kind, at, first_row, count, experts, rows)
        operands = [mine, arrived, weights, *sums, *more]
        return call(kernel, shapes, operands, scalars, 22 * 10**8)

    payload = pl.pallas_call(
        functools.partial(payload_kernel, experts),
        out_shape=jax.ShapeDtypeStruct((rows + EXTRA, width), BF16),
        in_specs=[pl.BlockSpec(memory_space=pltpu.HBM)] * 3,
        out_specs=pl.BlockSpec(memory_space=pltpu.VMEM),
        scratch_shapes=[
            pltpu.VMEM(routes.shape[::-1], jnp.int32),
            pltpu.VMEM(gates.shape[::-1], F32),
            pltpu.SemaphoreType.DMA((4,)),
        ],
        compiler_params=pltpu.CompilerParams(vmem_limit_bytes=VMEM_LIMIT),
        cost_estimate=pl.CostEstimate(flops=10**9, bytes_accessed=0, transcendentals=0),
    )(routes.T, gates.T, cotangent)
    tokens_now = tied((tokens,), (scalars,))[0]
    ring = [both_ways(tokens_now, tokens_now, "tok1"), both_ways(payload, payload, "cot1")]

    in_all, out_all = (w_in, swap_cores(w_in, "weights")), ()

    arrivals, outputs, lefts = [], [], []
    for turn in range(2 * steps):
        now = ring[turn]
        step = turn // 2 + 1
        name = ("tok", "cot")[turn % 2]
        sent = None
        if turn == 0:
            sent = call(
                first_tokens_kernel,
                [jax.ShapeDtypeStruct((2 * rows, width), BF16)],
                [*now, tokens, cotangent],
                scalars,
                2 * 10**9,
            )[0]
        elif turn == 1:
            seen = tied((*now, w_out), (*in_all, sent_first))
            cot_sent = pl.pallas_call(
                first_cotangent_kernel,
                out_shape=jax.ShapeDtypeStruct((rows + units, width), BF16),
                in_specs=[pl.BlockSpec(memory_space=pltpu.SMEM)]
                + [pl.BlockSpec(memory_space=pltpu.VMEM)] * 2
                + [pl.BlockSpec(memory_space=pltpu.HBM)],
                out_specs=pl.BlockSpec(memory_space=pltpu.VMEM),
                scratch_shapes=[pltpu.SemaphoreType.DMA((2,))],
                compiler_params=pltpu.CompilerParams(vmem_limit_bytes=VMEM_LIMIT),
                cost_estimate=pl.CostEstimate(flops=10**9, bytes_accessed=0, transcendentals=0),
            )(scalars, *seen)
            result, in_all = forward([("full", *arrivals[0])], in_all)
            outputs.append(result)
        elif turn < 2 * steps - 1:
            done = turn - 1
            first, second, other = arrivals[done]
            following = now if turn < 2 * steps - 3 else ()
            if turn == 2 * steps - 3:
                other = tied((other,), now)[0]
            pieces = [("full", first, second, other)]
            if done % 2 == 0:
                result, in_all = forward(pieces, in_all, following)
                if following:
                    *result, sent = result
                outputs.append(result)
            else:
                before = lefts if turn == 2 * steps - 2 else ()
                result, out_all = backward(
                    pieces, out_all, *outputs[done - 1], following, before
                )
                if following:
                    *result, sent = result
                lefts.append(result[0])
                outputs.append(result)
            if turn != 2 * steps - 3:
                now = tied(now, outputs[-1][:1])
        else:
            now = tied(now, outputs[-1])
        if turn == 0:
            sent_first = sent
        elif turn == 1:
            sent = cot_sent
        elif sent is None:
            sent = jnp.where(first_core, now[1], now[0])
        if step < steps - 1:
            ring.append(both_ways(now[0], now[1], name + str(step + 1)))
        elif step == steps - 1:
            cut = half + (EXTRA if turn % 2 else 0)
            ends = ring[turn][0][:cut], ring[turn][1][half:]
            ring.append(both_ways(*ends, name + str(step + 1)))
        other = swap_cores(sent, name + str(step))
        if turn == 0:
            own_arrived, other = other, other[:rows]
        elif turn == 1:
            out_all, other = (w_out, other), other[:rows]
        arrivals.append((*now, other))
    tok_pieces = [(rows, tokens, own_arrived), ("far", *arrivals[2 * steps - 2])]
    cot_pieces = [(rows + half, payload, own_arrived), ("far", *arrivals[2 * steps - 1])]
    lefts = lefts[-1]
    lefts_arrived = swap_cores(lefts, "lefts")
    hidden, slope = forward(tok_pieces, in_all)[0]
    ends = backward(cot_pieces, out_all, hidden, slope)[0][0]
    ends_arrived = swap_cores(ends, "ends")

    def weight_part(at, which, above, after):
        operands = [*above, lefts, lefts_arrived, ends, tied((ends_arrived,), after)[0]]
        for s in range(steps - 1):
            operands += arrivals[2 * s + which][:2]
        own, far_ends = (tok_pieces, cot_pieces)[which]
        operands += [own[1], *far_ends[1:3]]
        deep = local_units * (1 + len(above) // 2)
        return call(
            functools.partial(weight_kernel, at, rows),
            [jax.ShapeDtypeStruct((deep, width), BF16)] * 2,
            operands,
            scalars,
            2 * 10**9,
        )

    def over_groups(mine, other):
        if n_dp == 2:
            block = pl.BlockSpec((units // 4, width), lambda i: (i, 0))
            sent, kept = pl.pallas_call(
                send_kernel,
                grid=(4,),
                out_shape=[jax.ShapeDtypeStruct(mine.shape, BF16)] * 2,
                in_specs=[pl.BlockSpec(memory_space=pltpu.SMEM), block, block],
                out_specs=[block] * 2,
                compiler_params=pltpu.CompilerParams(vmem_limit_bytes=VMEM_LIMIT),
                cost_estimate=pl.CostEstimate(flops=10**9, bytes_accessed=0, transcendentals=0),
            )(scalars, mine, other)
            with jax.named_scope("groups"):
                return (sent,), kept, lax.ppermute(sent, "dp", [(0, 1), (1, 0)])
        part = jnp.concatenate([picked(core, mine, other), picked(core, other, mine)], axis=1)
        across = part.shape[1] // n_dp
        slices = [
            lax.dynamic_slice_in_dim(part, ((group + shift) % n_dp) * across, across, axis=1)
            for shift in range(n_dp)
        ]
        total = 0.0
        for shift in range(1, n_dp):
            pairs = [(i, (i + shift) % n_dp) for i in range(n_dp)]
            total = total + lax.ppermute(slices[shift], "dp", pairs).astype(F32)
        return (), slices[0], total

    def summed(kept, came):
        if n_dp != 2:
            total = kept.astype(F32) + came
            return total[:local_units], total[local_units:]
        tiles = 8
        return pl.pallas_call(
            add_kernel,
            out_shape=[jax.ShapeDtypeStruct((local_units, width), F32)] * 2,
            in_specs=[pl.BlockSpec(memory_space=pltpu.VMEM)] * 2,
            out_specs=[pl.BlockSpec(memory_space=pl.ANY)] * 2,
            scratch_shapes=[
                pltpu.VMEM((tiles, units // tiles, width), F32),
                pltpu.SemaphoreType.DMA((tiles,)),
            ],
            compiler_params=pltpu.CompilerParams(vmem_limit_bytes=VMEM_LIMIT),
            cost_estimate=pl.CostEstimate(flops=10**9, bytes_accessed=0, transcendentals=0),
        )(kept, came)

    def mixed_far(after):
        came = tied((ends_arrived,), after)[0]
        sent = returned("far", 0, half, ends, came, out_all[0], ())
        return sent, both_ways(sent[1], sent[0], "mixed")[::-1]

    def back_far(after):
        came = tied((ends_arrived,), after)[0]
        sent = returned("far", units, half, ends, came, in_all[0], ())
        return sent, both_ways(sent[1], sent[0], "grad")[::-1]

    def mixed_step(step, sums, after):
        kind = "join" if step == steps - 1 else "add"
        line = (step - 1) * rows
        sums = tied(sums, after)
        sent = returned(kind, 0, line, lefts, lefts_arrived, out_all[0], sums)
        return sent, both_ways(sent[1], sent[0], "mixed")[::-1]

    def back_step(step, sums, after):
        kind = "join" if step == steps - 1 else "add"
        line = (step - 1) * rows
        sums = tied(sums, after)
        sent = returned(kind, units, line, lefts, lefts_arrived, in_all[0], sums)
        return sent, both_ways(sent[1], sent[0], "grad")[::-1]

    part_out = weight_part(0, 1, (), ())
    parts, parts_other = weight_part(units, 0, part_out, ())
    parts_other = swap_cores(parts_other, "grad")
    sent, mixed_in = mixed_far((parts,))
    sent, back_in = back_far(sent)
    sent, mixed_in = mixed_step(steps - 1, mixed_in, sent)
    parts_sent, kept, came = over_groups(parts, tied((parts_other,), sent)[0])
    sent, back_in = back_step(steps - 1, back_in, (*sent, *parts_sent))
    for step in range(steps - 2, 0, -1):
        sent, mixed_in = mixed_step(step, mixed_in, sent)
        sent, back_in = back_step(step, back_in, sent)
    own = (0, ends, ends_arrived)
    mixed = returned("own", 0, *own, out_all[0], tied(mixed_in, sent))[0]
    grad_tokens, grad_gates = returned(
        "own", units, *own, in_all[0], tied(back_in, (mixed,)), (routes.T,)
    )
    grad_out, grad_in = summed(kept, tied((came,), (grad_tokens,))[0])
    return (mixed, grad_tokens, grad_gates.T, grad_in[None], grad_out[None])


def solution(mesh):
    placed = (
        P(("dp", "expert"), "tensor"),
        P(("dp", "expert"), None),
        P(("dp", "expert"), None),
        P("expert", "tensor", None),
        P("expert", "tensor", None),
        P(("dp", "expert"), "tensor"),
    )
    return jax.shard_map(
        per_device,
        mesh=mesh,
        in_specs=placed,
        out_specs=(
            P(("dp", "expert"), "tensor"),
            P(("dp", "expert"), "tensor"),
            P(("dp", "expert"), None),
            P("expert", "tensor", "dp"),
            P("expert", "tensor", "dp"),
        ),
        check_vma=False,
    )
```

```python
import functools

import jax
import jax.numpy as jnp
from jax import lax
from jax.experimental import pallas as pl
from jax.experimental.pallas import tpu as pltpu
from jax.sharding import PartitionSpec as P

BF16 = jnp.bfloat16
F32 = jnp.float32
VMEM_LIMIT = 16 * 1024 * 1024
LANES = 128
EXTRA = 16


def ring_order(count):
    if count % 2:
        return list(range(count))
    return list(range(0, count, 2)) + list(range(count - 1, 0, -2))


def swap_cores(value, name):
    with jax.named_scope("swap_" + name):
        return lax.ppermute(value, "tensor", [(0, 1), (1, 0)])


def tied(values, others):
    return lax.optimization_barrier((tuple(values), tuple(others)))[0]


def dot_width(rows, weights):
    return lax.dot_general(rows, weights, (((1,), (0,)), ((), ())), preferred_element_type=F32)


def dot_rows(left, right):
    return lax.dot_general(left, right, (((0,), (0,)), ((), ())), preferred_element_type=F32)


def call(kernel, out_shape, operands, scalars, work=4 * 10**9):
    return pl.pallas_call(
        kernel,
        out_shape=out_shape,
        in_specs=[pl.BlockSpec(memory_space=pltpu.SMEM)]
        + [pl.BlockSpec(memory_space=pltpu.VMEM)] * len(operands),
        out_specs=[pl.BlockSpec(memory_space=pltpu.VMEM)] * len(out_shape),
        compiler_params=pltpu.CompilerParams(vmem_limit_bytes=VMEM_LIMIT),
        cost_estimate=pl.CostEstimate(flops=work, bytes_accessed=0, transcendentals=0),
    )(scalars, *operands)


def picked(core, first, second):
    return jnp.where(core == 0, first, second)


def diagonal(count):
    across = lax.broadcasted_iota(jnp.int32, (count, count), 0)
    along = lax.broadcasted_iota(jnp.int32, (count, count), 1)
    return across == along


def column_of(row):
    return jnp.sum(jnp.where(diagonal(row.shape[1]), row, 0.0), axis=1, keepdims=True)


def row_of(column):
    return jnp.sum(jnp.where(diagonal(column.shape[0]), column, 0.0), axis=0, keepdims=True)


def pieces_of(value):
    high = value.astype(BF16).astype(F32)
    middle = (value - high).astype(BF16).astype(F32)
    return high, middle, value - high - middle


def prepare(core, local_ref, arrived_ref, flat_ref, mine_ref, other_ref):
    units, width = local_ref.shape[0], local_ref.shape[1] // 2
    at = pl.ds(pl.multiple_of(core * units, units), units)
    mine = pl.ds(pl.multiple_of(core * width, width), width)
    other = pl.ds(pl.multiple_of((1 - core) * width, width), width)
    block = local_ref[:, mine]
    flat_ref[at, :] = block
    mine_ref[:, at] = block.T
    other_ref[:, at] = local_ref[:, other].T
    came = pl.ds(pl.multiple_of((1 - core) * units, units), units)
    if arrived_ref.shape[1] > width:
        block, beside = arrived_ref[:, mine], arrived_ref[:, other]
    else:
        start = arrived_ref.shape[0] - 2 * units
        mine = pl.ds(pl.multiple_of(start + core * units, LANES), units)
        other = pl.ds(pl.multiple_of(start + (1 - core) * units, LANES), units)
        block, beside = arrived_ref[mine, :], arrived_ref[other, :]
    flat_ref[came, :] = block
    mine_ref[:, came] = block.T
    other_ref[:, came] = beside.T


def stacked(values):
    return jnp.concatenate(values, axis=0) if len(values) > 1 else values[0]


def table_parts(expert, rows, width, experts):
    per_row = width // rows
    deep = -(-experts // per_row)
    line = lax.broadcasted_iota(jnp.int32, (EXTRA, width), 0)
    lane = lax.broadcasted_iota(jnp.int32, (EXTRA, width), 1)
    lanes = lane // rows == lax.rem(expert, per_row)
    return [lanes & (line == i * deep + expert // per_row) for i in range(3)]


def payload_kernel(experts, routes_hbm, gates_hbm, cotangent_hbm, out_ref, routes_ref, gates_ref, sems):
    rows, width = cotangent_hbm.shape
    half = rows // 2
    copies = [
        pltpu.make_async_copy(routes_hbm, routes_ref, sems.at[0]),
        pltpu.make_async_copy(gates_hbm, gates_ref, sems.at[1]),
        pltpu.make_async_copy(
            cotangent_hbm.at[pl.ds(0, half), :], out_ref.at[pl.ds(0, half), :], sems.at[2]
        ),
        pltpu.make_async_copy(
            cotangent_hbm.at[pl.ds(half, half), :],
            out_ref.at[pl.ds(half + EXTRA, half), :],
            sems.at[3],
        ),
    ]
    for copy in copies:
        copy.start()
    copies[0].wait()
    copies[1].wait()
    table = jnp.zeros((EXTRA, width), F32)
    for expert in range(experts):
        named = jnp.where(routes_ref[...] == expert, gates_ref[...], 0.0)
        row = jnp.sum(named, axis=0, keepdims=True)
        for piece, place in zip(pieces_of(row), table_parts(expert, rows, width, experts)):
            spread = jnp.concatenate([piece] * (width // rows), axis=1)
            table = jnp.where(place, spread, table)
    out_ref[half : half + EXTRA, :] = table.astype(BF16)
    copies[2].wait()
    copies[3].wait()


def gate_column(extra, expert, rows, experts):
    width = extra.shape[1]
    places = table_parts(expert, rows, width, experts)
    values = extra.astype(F32)
    row = sum(jnp.sum(jnp.where(p, values, 0.0), axis=0, keepdims=True) for p in places)
    row = sum(row[:, i * rows : (i + 1) * rows] for i in range(width // rows))
    return column_of(row)


def first_tokens_kernel(scalars, first, second, out_ref):
    out_ref[...] = picked(scalars[0], second[...], first[...])


def first_cotangent_kernel(scalars, first, second, tokens, cotangent, w_ref, out_ref, sems):
    core = scalars[0]
    units, width = w_ref.shape[0], out_ref.shape[1]
    rows, half = first.shape[0], tokens.shape[0] // 2
    start = out_ref.shape[0] - 2 * units
    copies = [
        pltpu.make_async_copy(
            w_ref.at[:, pl.ds(i * width, width)],
            out_ref.at[pl.ds(start + i * units, units), :],
            sems.at[i],
        )
        for i in range(2)
    ]
    for copy in copies:
        copy.start()
    out_ref[:rows, :] = picked(core, second[...], first[...])
    for i, ref in enumerate((tokens, cotangent)):
        at = rows + i * half
        out_ref[at : at + half, :] = picked(core, ref[half:, :], ref[:half, :])
    for copy in copies:
        copy.wait()


def whole_kernel(scalars, first, second, other, out_ref):
    rows, width = first.shape
    out_ref[:, :width] = picked(scalars[0], first[...], second[...])
    out_ref[:, width:] = other[:rows, :]


def taken(kinds, refs):
    pieces = []
    for kind in kinds:
        count = 2 if isinstance(kind, int) else 1
        pieces.append((kind, refs[:count]))
        refs = refs[count:]
    return pieces, refs


def rows_of(core, piece, rows, width):
    kind, refs = piece
    half = rows // 2
    if isinstance(kind, int):
        block, arrived = refs
        there = arrived[kind : kind + half, :]
        if block.shape[0] == rows:
            return picked(core, block[:half, :], block[half:, :]), there, None
        here = picked(core, block[:half, :], block[half + EXTRA :, :])
        return here, there, block[half : half + EXTRA, :]
    (block,) = refs
    count = block.shape[0]
    if count in (rows, half):
        lines, extra = block[...], None
    elif count > rows:
        lines = stacked([block[:half, :], block[half + EXTRA :, :]])
        extra = block[half : half + EXTRA, :width]
    else:
        lines = picked(core, block[:half, :], block[EXTRA:, :])
        extra = picked(core, block[half:, :width], block[:EXTRA, :width])
    return lines[:, :width], lines[:, width:], extra


def units_of(core, pieces, rows, w_ref, w_other_ref):
    width = w_ref.shape[0]
    here, there, extra = zip(*(rows_of(core, p, rows, width) for p in pieces))
    wide = dot_width(stacked(here), w_ref[...]) + dot_width(stacked(there), w_other_ref[...])
    return wide, extra


def forward_kernel(kinds, rows, with_weights, scalars, *refs):
    core = scalars[0]
    if with_weights:
        weights = refs[-2:]
        prepare(core, *refs[:2], *refs[-3:])
        refs = refs[2:-3]
    hidden_ref, slope_ref = refs[-2:]
    pieces, refs = taken(kinds, refs)
    if not with_weights:
        weights = refs[:2]
    pre = units_of(core, pieces, rows, *weights)[0]
    logistic = 1.0 / (1.0 + jnp.exp(-pre))
    hidden_ref[...] = (pre * logistic).astype(BF16)
    slope_ref[...] = logistic * (1.0 + pre * (1.0 - logistic))


def backward_kernel(kinds, rows, experts, with_weights, before, scalars, *refs):
    core, expert = scalars[0], scalars[1]
    if with_weights:
        weights = refs[-2:]
        prepare(core, *refs[:2], *refs[-3:])
        refs = refs[2:-3]
    if before:
        lines = refs[0].shape[0]
        for i in range(before):
            refs[-1][i * lines : (i + 1) * lines, :] = refs[i][...]
        refs = (*refs[before:-1], refs[-1].at[before * lines :, :])
    hidden_ref, slope_ref, out_ref = refs[-3:]
    pieces, refs = taken(kinds, refs)
    if not with_weights:
        weights = refs[:2]
    lines, units = hidden_ref.shape
    wide, extras = units_of(core, pieces, rows, *weights)
    columns = []
    for extra in extras:
        column = gate_column(extra, expert, rows, experts)
        if len(kinds) > 1:
            column = picked(core, column[: rows // 2], column[rows // 2 :])
        columns.append(column)
    gate = stacked(columns)
    hidden = hidden_ref[...].astype(F32)
    out_ref[:, :units] = (gate * hidden).astype(BF16)
    out_ref[:, units : 2 * units] = (gate * slope_ref[...] * wide).astype(BF16)
    sums = jnp.sum(hidden * wide, axis=1, keepdims=True)
    lane = lax.broadcasted_iota(jnp.int32, (lines, LANES), 1)
    kept = jnp.zeros((lines, LANES), F32)
    for i, piece in enumerate(pieces_of(sums)):
        kept = jnp.where(lane == i, piece, kept)
    out_ref[:, 2 * units : 2 * units + LANES] = kept.astype(BF16)


def dots_rows(expert, dots, start, rows, width, experts):
    count = dots.shape[0]
    row = row_of(dots)
    if count < rows:
        blank = jnp.zeros((1, count), F32)
        row = jnp.concatenate([row, blank] if start == 0 else [blank, row], axis=1)
    out = jnp.zeros((EXTRA, width), F32)
    for piece, place in zip(pieces_of(row), table_parts(expert, rows, width, experts)):
        out = jnp.where(place, jnp.concatenate([piece] * (width // rows), axis=1), out)
    return out


def return_kernel(kind, at, first_row, count, experts, rows, scalars, mine_ref, arrived_ref, w_ref, *refs):
    core, expert = scalars[0], scalars[1]
    units, width = w_ref.shape
    lanes = slice(at, at + units + (LANES if at else 0))
    mine_all = mine_ref[first_row : first_row + count, lanes]
    arrived_all = arrived_ref[first_row : first_row + count, lanes]
    mine, arrived = mine_all[:, :units], arrived_all[:, :units]
    both = jnp.concatenate([picked(core, mine, arrived), picked(core, arrived, mine)], axis=0)
    part = dot_width(both, w_ref[...])
    with_dots = at > 0
    extra = [None, None]
    if with_dots:
        mine = jnp.sum(mine_all[:, units:].astype(F32), axis=1, keepdims=True)
        arrived = jnp.sum(arrived_all[:, units:].astype(F32), axis=1, keepdims=True)
        dots = [picked(core, mine, arrived), picked(core, arrived, mine)]
        starts = (0, count if count < rows else 0)
        extra = [
            dots_rows(expert, d, start, rows, width, experts) for d, start in zip(dots, starts)
        ]
    if kind == "far":
        for i, out_ref in enumerate(refs):
            out_ref[:count, :] = part[i * count : (i + 1) * count].astype(BF16)
            if with_dots:
                out_ref[count:, :] = extra[i].astype(BF16)
        return
    from_ahead, from_behind = refs[:2]
    if kind == "own":
        total = part + from_ahead[:rows, :].astype(F32) + from_behind[:rows, :].astype(F32)
        if not with_dots:
            refs[2][...] = total.astype(BF16)
            return
        routes_ref, out_ref, gates_ref = refs[2:]
        out_ref[...] = total.astype(BF16)
        table = extra[0] + extra[1]
        table = table + from_ahead[rows:, :].astype(F32) + from_behind[rows:, :].astype(F32)
        per_row = width // rows
        deep = -(-experts // per_row)
        routes = routes_ref[...]
        grads = jnp.zeros(routes.shape, F32)
        for e in range(experts):
            lanes = slice((e % per_row) * rows, (e % per_row + 1) * rows)
            line = e // per_row
            row = sum(table[i * deep + line : i * deep + line + 1, lanes] for i in range(3))
            grads = jnp.where(routes == e, row, grads)
        gates_ref[...] = grads
        return
    behind_ref, ahead_ref = refs[2:]
    behind, ahead = part[:count], part[count:]
    if kind == "join":
        half = count // 2
        behind_ref[:half, :] = (behind[:half] + from_ahead[:half, :].astype(F32)).astype(BF16)
        behind_ref[half:count, :] = behind[half:].astype(BF16)
        ahead_ref[:half, :] = ahead[:half].astype(BF16)
        ahead_ref[half:count, :] = (ahead[half:] + from_behind[:half, :].astype(F32)).astype(BF16)
    else:
        half = count
        behind_ref[:count, :] = (behind + from_ahead[:count, :].astype(F32)).astype(BF16)
        ahead_ref[:count, :] = (ahead + from_behind[:count, :].astype(F32)).astype(BF16)
    if with_dots:
        behind_ref[count:, :] = (extra[0] + from_ahead[half:, :].astype(F32)).astype(BF16)
        ahead_ref[count:, :] = (extra[1] + from_behind[half:, :].astype(F32)).astype(BF16)


def weight_kernel(blocks, rows, scalars, *refs):
    core = scalars[0]
    above, ends, own_other = refs[:3]
    own_ref, other_ref = refs[-2:]
    units, width = own_ref.shape[0] // 4, own_ref.shape[1]
    for i in range(2):
        lanes = slice(2 * i * units, 2 * (i + 1) * units)
        left = stacked([above[:, lanes], ends[:, lanes]])
        pieces = [("block", (ref,)) for ref in refs[3 + i * blocks : 3 + (i + 1) * blocks]]
        first_row = rows + EXTRA + (1 - i) * (rows // 2)
        pieces[-2] = (first_row, (pieces[-2][1][0], own_other))
        here, there, _ = zip(*(rows_of(core, p, rows, width) for p in pieces))
        for side, right in enumerate((here, there)):
            part = dot_rows(left, stacked(right))
            own = picked(core, part[:units], part[units:]).astype(BF16)
            other = picked(core, part[units:], part[:units]).astype(BF16)
            kept = jnp.where(scalars[2] == side, 1, 0)
            at = pl.ds(pl.multiple_of(kept * 2 * units + i * units, units), units)
            own_ref[at, :] = own
            other_ref[at, :] = other


def send_kernel(own_ref, came_ref, out_ref):
    out_ref[...] = (own_ref[...].astype(F32) + came_ref[...].astype(F32)).astype(BF16)


def add_kernel(own_ref, other_ref, came_ref, first_hbm, second_hbm, held_ref, sems):
    tiles, rows = held_ref.shape[0], held_ref.shape[1]
    copies = []
    for i in range(tiles):
        at = slice(i * rows, (i + 1) * rows)
        below = slice((tiles + i) * rows, (tiles + i + 1) * rows)
        kept = own_ref[below, :].astype(F32) + other_ref[below, :].astype(F32)
        held_ref[i] = kept + came_ref[at, :].astype(F32)
        out = first_hbm if i < tiles // 2 else second_hbm
        start = (i % (tiles // 2)) * rows
        copy = pltpu.make_async_copy(held_ref.at[i], out.at[pl.ds(start, rows), :], sems.at[i])
        copy.start()
        copies.append(copy)
    for copy in copies:
        copy.wait()


def per_device(tokens, routes, gates, w_in, w_out, cotangent):
    size = lax.axis_size("expert")
    n_dp = lax.axis_size("dp")
    rows, width = tokens.shape
    half = rows // 2
    experts = size * w_in.shape[0]
    core = lax.axis_index("tensor")
    place = lax.axis_index("expert")
    group = lax.axis_index("dp")
    order = ring_order(size)
    onward_pairs = [(order[i], order[(i + 1) % size]) for i in range(size)]
    back_pairs = [(b, a) for a, b in onward_pairs]
    steps = size // 2
    w_in, w_out = w_in[0], w_out[0]
    local_units = w_in.shape[0]
    units = 2 * local_units

    def both_ways(forth_value, back_value, name):
        with jax.named_scope("onward_" + name):
            forth = lax.ppermute(forth_value, "expert", onward_pairs)
        with jax.named_scope("back_" + name):
            return forth, lax.ppermute(back_value, "expert", back_pairs)

    first_core = lax.optimization_barrier(core == 0)
    core_now = jnp.where(first_core, 0, 1)
    scalars = jnp.stack([core_now, place, (core + group) % 2]).astype(jnp.int32)

    weight_shapes = [
        jax.ShapeDtypeStruct((units, width), BF16),
        jax.ShapeDtypeStruct((width, units), BF16),
        jax.ShapeDtypeStruct((width, units), BF16),
    ]

    def split(pieces):
        return tuple(p[0] for p in pieces), [v for p in pieces for v in p[1:]]

    def forward(pieces, weights):
        shape = (rows, units)
        raw = weights[0] is w_in
        kinds, operands = split(pieces)
        result = call(
            functools.partial(forward_kernel, kinds, rows, raw),
            [
                jax.ShapeDtypeStruct(shape, BF16),
                jax.ShapeDtypeStruct(shape, F32),
                *(weight_shapes if raw else ()),
            ],
            [*(weights if raw else ()), *operands, *(() if raw else weights[1:])],
            scalars,
            10**9,
        )
        return (result[:-3], result[-3:]) if raw else (result, weights)

    def backward(pieces, weights, hidden, slope, before=()):
        count = hidden.shape[0] * (1 + len(before))
        raw = weights[0] is w_out
        kinds, operands = split(pieces)
        result = call(
            functools.partial(backward_kernel, kinds, rows, experts, raw, len(before)),
            [
                jax.ShapeDtypeStruct((count, 2 * units + LANES), BF16),
                *(weight_shapes if raw else ()),
            ],
            [
                *(weights if raw else ()),
                *before,
                *operands,
                *(() if raw else weights[1:]),
                hidden,
                slope,
            ],
            scalars,
            10**9,
        )
        return (result[:-3], result[-3:]) if raw else (result, weights)

    def returned(kind, at, first_row, mine, arrived, weights, sums, more=()):
        count = rows if kind in ("join", "add") else half
        extra = EXTRA if at else 0
        if kind == "own":
            shapes = [jax.ShapeDtypeStruct((rows, width), BF16)]
            if at:
                shapes.append(jax.ShapeDtypeStruct(routes.shape[::-1], F32))
        else:
            shapes = [jax.ShapeDtypeStruct((count + extra, width), BF16)] * 2
        kernel = functools.partial(return_kernel, kind, at, first_row, count, experts, rows)
        operands = [mine, arrived, weights, *sums, *more]
        return call(kernel, shapes, operands, scalars, 22 * 10**8)

    apart_pairs = [(2 * i, 2 * j) for i, j in onward_pairs]
    apart_pairs += [(2 * i + 1, 2 * j + 1) for i, j in back_pairs]

    def apart(value, name):
        with jax.named_scope("onward_" + name):
            return lax.ppermute(value, ("expert", "tensor"), apart_pairs)

    payload = pl.pallas_call(
        functools.partial(payload_kernel, experts),
        out_shape=jax.ShapeDtypeStruct((rows + EXTRA, width), BF16),
        in_specs=[pl.BlockSpec(memory_space=pltpu.HBM)] * 3,
        out_specs=pl.BlockSpec(memory_space=pltpu.VMEM),
        scratch_shapes=[
            pltpu.VMEM(routes.shape[::-1], jnp.int32),
            pltpu.VMEM(gates.shape[::-1], F32),
            pltpu.SemaphoreType.DMA((4,)),
        ],
        compiler_params=pltpu.CompilerParams(vmem_limit_bytes=VMEM_LIMIT),
        cost_estimate=pl.CostEstimate(flops=10**9, bytes_accessed=0, transcendentals=0),
    )(routes.T, gates.T, cotangent)
    tokens_now = tied((tokens,), (scalars,))[0]
    ring = [both_ways(tokens_now, tokens_now, "tok1"), both_ways(payload, payload, "cot1")]

    in_all, out_all = (w_in, swap_cores(w_in, "weights")), ()

    tok_sent = call(
        first_tokens_kernel,
        [jax.ShapeDtypeStruct((rows, width), BF16)],
        [*ring[0]],
        scalars,
        2 * 10**9,
    )[0]
    tok_came = swap_cores(tok_sent, "tok1")
    def whole(pair, other):
        count = pair[0].shape[0]
        shape = [jax.ShapeDtypeStruct((count, 2 * width), BF16)]
        return call(whole_kernel, shape, [*pair, other], scalars, 10**6)[0]

    tok_whole = whole(ring[0], tok_came)
    seen = tied((*ring[1], w_out), (*in_all, tok_whole))
    cot_sent = pl.pallas_call(
        first_cotangent_kernel,
        out_shape=jax.ShapeDtypeStruct((2 * rows + EXTRA + units, width), BF16),
        in_specs=[pl.BlockSpec(memory_space=pltpu.SMEM)]
        + [pl.BlockSpec(memory_space=pltpu.VMEM)] * 4
        + [pl.BlockSpec(memory_space=pltpu.HBM)],
        out_specs=pl.BlockSpec(memory_space=pltpu.VMEM),
        scratch_shapes=[pltpu.SemaphoreType.DMA((2,))],
        compiler_params=pltpu.CompilerParams(vmem_limit_bytes=VMEM_LIMIT),
        cost_estimate=pl.CostEstimate(flops=10**9, bytes_accessed=0, transcendentals=0),
    )(scalars, *seen[:2], tokens, cotangent, seen[2])
    own_arrived = swap_cores(cot_sent, "cot1")
    out_all = (w_out, own_arrived)

    arrivals = [tok_whole, whole(ring[1], out_all[1])]
    outputs, lefts = [], []
    for turn in range(2 * steps):
        step = turn // 2 + 1
        name = ("tok", "cot")[turn % 2] + str(step + 1)
        now = arrivals[turn]
        if turn >= 2:
            now = arrivals[turn] = tied((now,), outputs[turn - 2])[0]
        if step < steps - 1:
            arrivals.append(apart(now, name))
        elif step == steps - 1:
            cut = half + (EXTRA if turn % 2 else 0)
            arrivals.append(apart(jnp.where(first_core, now[:cut], now[half:]), name))
        pieces = [("block", now)]
        if turn % 2 == 0:
            if step == steps:
                pieces = [(rows + EXTRA, tokens, own_arrived), *pieces]
            result, in_all = forward(pieces, in_all)
        else:
            if step == steps:
                pieces = [(rows + EXTRA + half, payload, own_arrived), *pieces]
            before = lefts if step == steps - 1 else ()
            result, out_all = backward(pieces, out_all, *outputs[-1], before)
            lefts.append(result[0])
        outputs.append(result)
    ends = lefts[steps - 1]
    lefts = lefts[steps - 2]
    lefts_arrived = swap_cores(tied((lefts,), (ends,))[0], "lefts")
    ends_arrived = swap_cores(ends, "ends")

    def weight_parts(after):
        operands = [lefts, tied((ends,), after)[0], own_arrived]
        for which in (1, 0):
            blocks = [arrivals[2 * step + which] for step in range(steps)]
            own = (tokens, payload)[which]
            operands += [*blocks[:-1], own, blocks[-1]]
        return pl.pallas_call(
            functools.partial(weight_kernel, steps + 1, rows),
            out_shape=[jax.ShapeDtypeStruct((2 * units, width), BF16)] * 2,
            in_specs=[pl.BlockSpec(memory_space=pltpu.SMEM)]
            + [pl.BlockSpec(memory_space=pltpu.VMEM)] * len(operands),
            out_specs=[pl.BlockSpec(memory_space=pltpu.VMEM)] * 2,
            compiler_params=pltpu.CompilerParams(vmem_limit_bytes=2 * VMEM_LIMIT),
            cost_estimate=pl.CostEstimate(flops=4 * 10**9, bytes_accessed=0, transcendentals=0),
        )(scalars, *operands)

    def over_groups(own, came):
        block = pl.BlockSpec((units // 4, width), lambda i: (i, 0))
        sent = pl.pallas_call(
            send_kernel,
            grid=(4,),
            out_shape=jax.ShapeDtypeStruct((units, width), BF16),
            in_specs=[block] * 2,
            out_specs=block,
            compiler_params=pltpu.CompilerParams(vmem_limit_bytes=VMEM_LIMIT),
            cost_estimate=pl.CostEstimate(flops=10**9, bytes_accessed=0, transcendentals=0),
        )(own, came)
        with jax.named_scope("groups"):
            return (sent,), lax.ppermute(sent, "dp", [(0, 1), (1, 0)])

    def over_many_groups(away, kept):
        mine = picked((core + group) % 2, kept, away)
        other = picked((core + group) % 2, away, kept)
        part = jnp.concatenate([picked(core, mine, other), picked(core, other, mine)], axis=1)
        across = part.shape[1] // n_dp
        slices = [
            lax.dynamic_slice_in_dim(part, ((group + shift) % n_dp) * across, across, axis=1)
            for shift in range(n_dp)
        ]
        total = slices[0]
        for shift in range(1, n_dp):
            pairs = [(i, (i + shift) % n_dp) for i in range(n_dp)]
            total = total + lax.ppermute(slices[shift].astype(BF16), "dp", pairs).astype(F32)
        return total[:local_units], total[local_units:]

    def summed(own, kept, came):
        tiles = 8
        return pl.pallas_call(
            add_kernel,
            out_shape=[jax.ShapeDtypeStruct((local_units, width), F32)] * 2,
            in_specs=[pl.BlockSpec(memory_space=pltpu.VMEM)] * 3,
            out_specs=[pl.BlockSpec(memory_space=pl.ANY)] * 2,
            scratch_shapes=[
                pltpu.VMEM((tiles, units // tiles, width), F32),
                pltpu.SemaphoreType.DMA((tiles,)),
            ],
            compiler_params=pltpu.CompilerParams(vmem_limit_bytes=VMEM_LIMIT),
            cost_estimate=pl.CostEstimate(flops=10**9, bytes_accessed=0, transcendentals=0),
        )(own, kept, came)

    def mixed_far(after):
        came = tied((ends_arrived,), after)[0]
        sent = returned("far", 0, half, ends, came, out_all[0], ())
        return sent, both_ways(sent[1], sent[0], "mixed")[::-1]

    def back_far(after):
        came = tied((ends_arrived,), after)[0]
        sent = returned("far", units, half, ends, came, in_all[0], ())
        return sent, both_ways(sent[1], sent[0], "grad")[::-1]

    def mixed_step(step, sums, after):
        kind = "join" if step == steps - 1 else "add"
        line = (step - 1) * rows
        sums = tied(sums, after)
        sent = returned(kind, 0, line, lefts, lefts_arrived, out_all[0], sums)
        return sent, both_ways(sent[1], sent[0], "mixed")[::-1]

    def back_step(step, sums, after):
        kind = "join" if step == steps - 1 else "add"
        line = (step - 1) * rows
        sums = tied(sums, after)
        sent = returned(kind, units, line, lefts, lefts_arrived, in_all[0], sums)
        return sent, both_ways(sent[1], sent[0], "grad")[::-1]

    parts, parts_other = weight_parts(())
    sent, mixed_in = mixed_far((parts, lefts_arrived))
    parts_came = swap_cores(tied((parts_other,), sent)[0], "parts")
    sent, back_in = back_far(sent)
    sent, mixed_in = mixed_step(steps - 1, mixed_in, sent)
    after = sent
    if n_dp == 2:
        parts_sent, came = over_groups(parts, tied((parts_came,), sent)[0])
        after = (*sent, *parts_sent)
    sent, back_in = back_step(steps - 1, back_in, after)
    for step in range(steps - 2, 0, -1):
        sent, mixed_in = mixed_step(step, mixed_in, sent)
        sent, back_in = back_step(step, back_in, sent)
    own = (0, ends, ends_arrived)
    mixed = returned("own", 0, *own, out_all[0], tied(mixed_in, sent))[0]
    grad_tokens, grad_gates = returned(
        "own", units, *own, in_all[0], tied(back_in, (mixed,)), (routes.T,)
    )
    if n_dp == 2:
        came = tied((came,), (grad_tokens,))[0]
        grad_out, grad_in = summed(parts, parts_came, came)
    else:
        both = parts.astype(F32) + parts_came.astype(F32)
        grad_out, grad_in = over_many_groups(both[:units], both[units:])
    return (mixed, grad_tokens, grad_gates.T, grad_in[None], grad_out[None])


def solution(mesh):
    placed = (
        P(("dp", "expert"), "tensor"),
        P(("dp", "expert"), None),
        P(("dp", "expert"), None),
        P("expert", "tensor", None),
        P("expert", "tensor", None),
        P(("dp", "expert"), "tensor"),
    )
    return jax.shard_map(
        per_device,
        mesh=mesh,
        in_specs=placed,
        out_specs=(
            P(("dp", "expert"), "tensor"),
            P(("dp", "expert"), "tensor"),
            P(("dp", "expert"), None),
            P("expert", "tensor", "dp"),
            P("expert", "tensor", "dp"),
        ),
        check_vma=False,
    )
```

```python
import functools

import jax
import jax.numpy as jnp
from jax import lax
from jax.experimental import pallas as pl
from jax.experimental.pallas import tpu as pltpu
from jax.sharding import PartitionSpec as P

BF16 = jnp.bfloat16
F32 = jnp.float32
VMEM_LIMIT = 16 * 1024 * 1024
LANES = 128
EXTRA = 16


def ring_order(count):
    if count % 2:
        return list(range(count))
    return list(range(0, count, 2)) + list(range(count - 1, 0, -2))


def swap_cores(value, name):
    with jax.named_scope("swap_" + name):
        return lax.ppermute(value, "tensor", [(0, 1), (1, 0)])


def tied(values, others):
    return lax.optimization_barrier((tuple(values), tuple(others)))[0]


def dot_width(rows, weights):
    return lax.dot_general(rows, weights, (((1,), (0,)), ((), ())), preferred_element_type=F32)


def dot_rows(left, right):
    return lax.dot_general(left, right, (((0,), (0,)), ((), ())), preferred_element_type=F32)


def call(kernel, out_shape, operands, scalars, work=4 * 10**9):
    return pl.pallas_call(
        kernel,
        out_shape=out_shape,
        in_specs=[pl.BlockSpec(memory_space=pltpu.SMEM)]
        + [pl.BlockSpec(memory_space=pltpu.VMEM)] * len(operands),
        out_specs=[pl.BlockSpec(memory_space=pltpu.VMEM)] * len(out_shape),
        compiler_params=pltpu.CompilerParams(vmem_limit_bytes=VMEM_LIMIT),
        cost_estimate=pl.CostEstimate(flops=work, bytes_accessed=0, transcendentals=0),
    )(scalars, *operands)


def picked(core, first, second):
    return jnp.where(core == 0, first, second)


def diagonal(count):
    across = lax.broadcasted_iota(jnp.int32, (count, count), 0)
    along = lax.broadcasted_iota(jnp.int32, (count, count), 1)
    return across == along


def column_of(row):
    return jnp.sum(jnp.where(diagonal(row.shape[1]), row, 0.0), axis=1, keepdims=True)


def row_of(column):
    return jnp.sum(jnp.where(diagonal(column.shape[0]), column, 0.0), axis=0, keepdims=True)


def pieces_of(value):
    high = value.astype(BF16).astype(F32)
    middle = (value - high).astype(BF16).astype(F32)
    return high, middle, value - high - middle


def prepare(core, local_ref, arrived_ref, flat_ref, mine_ref, other_ref):
    units, width = local_ref.shape[0], local_ref.shape[1] // 2
    at = pl.ds(pl.multiple_of(core * units, units), units)
    mine = pl.ds(pl.multiple_of(core * width, width), width)
    other = pl.ds(pl.multiple_of((1 - core) * width, width), width)
    block = local_ref[:, mine]
    flat_ref[at, :] = block
    mine_ref[:, at] = block.T
    other_ref[:, at] = local_ref[:, other].T
    came = pl.ds(pl.multiple_of((1 - core) * units, units), units)
    if arrived_ref.shape[1] > width:
        block, beside = arrived_ref[:, mine], arrived_ref[:, other]
    else:
        start = arrived_ref.shape[0] - 2 * units
        mine = pl.ds(pl.multiple_of(start + core * units, LANES), units)
        other = pl.ds(pl.multiple_of(start + (1 - core) * units, LANES), units)
        block, beside = arrived_ref[mine, :], arrived_ref[other, :]
    flat_ref[came, :] = block
    mine_ref[:, came] = block.T
    other_ref[:, came] = beside.T


def stacked(values):
    return jnp.concatenate(values, axis=0) if len(values) > 1 else values[0]


def table_parts(expert, rows, width, experts):
    per_row = width // rows
    deep = -(-experts // per_row)
    line = lax.broadcasted_iota(jnp.int32, (EXTRA, width), 0)
    lane = lax.broadcasted_iota(jnp.int32, (EXTRA, width), 1)
    lanes = lane // rows == lax.rem(expert, per_row)
    return [lanes & (line == i * deep + expert // per_row) for i in range(3)]


def payload_kernel(experts, routes_hbm, gates_hbm, cotangent_hbm, out_ref, routes_ref, gates_ref, sems):
    rows, width = cotangent_hbm.shape
    half = rows // 2
    copies = [
        pltpu.make_async_copy(routes_hbm, routes_ref, sems.at[0]),
        pltpu.make_async_copy(gates_hbm, gates_ref, sems.at[1]),
        pltpu.make_async_copy(
            cotangent_hbm.at[pl.ds(0, half), :], out_ref.at[pl.ds(0, half), :], sems.at[2]
        ),
        pltpu.make_async_copy(
            cotangent_hbm.at[pl.ds(half, half), :],
            out_ref.at[pl.ds(half + EXTRA, half), :],
            sems.at[3],
        ),
    ]
    for copy in copies:
        copy.start()
    copies[0].wait()
    copies[1].wait()
    table = jnp.zeros((EXTRA, width), F32)
    for expert in range(experts):
        named = jnp.where(routes_ref[...] == expert, gates_ref[...], 0.0)
        row = jnp.sum(named, axis=0, keepdims=True)
        for piece, place in zip(pieces_of(row), table_parts(expert, rows, width, experts)):
            spread = jnp.concatenate([piece] * (width // rows), axis=1)
            table = jnp.where(place, spread, table)
    out_ref[half : half + EXTRA, :] = table.astype(BF16)
    copies[2].wait()
    copies[3].wait()


def gate_column(extra, expert, rows, experts):
    width = extra.shape[1]
    places = table_parts(expert, rows, width, experts)
    values = extra.astype(F32)
    row = sum(jnp.sum(jnp.where(p, values, 0.0), axis=0, keepdims=True) for p in places)
    row = sum(row[:, i * rows : (i + 1) * rows] for i in range(width // rows))
    return column_of(row)


def first_tokens_kernel(scalars, first, second, out_ref):
    out_ref[...] = picked(scalars[0], second[...], first[...])


def first_cotangent_kernel(scalars, first, second, tokens, cotangent, w_ref, out_ref, sems):
    core = scalars[0]
    units, width = w_ref.shape[0], out_ref.shape[1]
    rows, half = first.shape[0], tokens.shape[0] // 2
    start = out_ref.shape[0] - 2 * units
    copies = [
        pltpu.make_async_copy(
            w_ref.at[:, pl.ds(i * width, width)],
            out_ref.at[pl.ds(start + i * units, units), :],
            sems.at[i],
        )
        for i in range(2)
    ]
    for copy in copies:
        copy.start()
    out_ref[:rows, :] = picked(core, second[...], first[...])
    for i, ref in enumerate((tokens, cotangent)):
        at = rows + i * half
        out_ref[at : at + half, :] = picked(core, ref[half:, :], ref[:half, :])
    for copy in copies:
        copy.wait()


def whole_kernel(scalars, first, second, other, out_ref):
    rows, width = first.shape
    out_ref[:, :width] = picked(scalars[0], first[...], second[...])
    out_ref[:, width:] = other[:rows, :]


def taken(kinds, refs):
    pieces = []
    for kind in kinds:
        count = 2 if isinstance(kind, int) else 1
        pieces.append((kind, refs[:count]))
        refs = refs[count:]
    return pieces, refs


def rows_of(core, piece, rows, width):
    kind, refs = piece
    half = rows // 2
    if isinstance(kind, int):
        block, arrived = refs
        there = arrived[kind : kind + half, :]
        if block.shape[0] == rows:
            return picked(core, block[:half, :], block[half:, :]), there, None
        here = picked(core, block[:half, :], block[half + EXTRA :, :])
        return here, there, block[half : half + EXTRA, :]
    (block,) = refs
    count = block.shape[0]
    if count in (rows, half):
        lines, extra = block[...], None
    elif count > rows:
        lines = stacked([block[:half, :], block[half + EXTRA :, :]])
        extra = block[half : half + EXTRA, :width]
    else:
        lines = picked(core, block[:half, :], block[EXTRA:, :])
        extra = picked(core, block[half:, :width], block[:EXTRA, :width])
    return lines[:, :width], lines[:, width:], extra


def units_of(core, pieces, rows, w_ref, w_other_ref):
    width = w_ref.shape[0]
    here, there, extra = zip(*(rows_of(core, p, rows, width) for p in pieces))
    wide = dot_width(stacked(here), w_ref[...]) + dot_width(stacked(there), w_other_ref[...])
    return wide, extra


def forward_kernel(kinds, rows, with_weights, scalars, *refs):
    core = scalars[0]
    if with_weights:
        weights = refs[-2:]
        prepare(core, *refs[:2], *refs[-3:])
        refs = refs[2:-3]
    hidden_ref, slope_ref = refs[-2:]
    pieces, refs = taken(kinds, refs)
    if not with_weights:
        weights = refs[:2]
    pre = units_of(core, pieces, rows, *weights)[0]
    logistic = 1.0 / (1.0 + jnp.exp(-pre))
    hidden_ref[...] = (pre * logistic).astype(BF16)
    slope_ref[...] = logistic * (1.0 + pre * (1.0 - logistic))


def backward_kernel(kinds, rows, experts, with_weights, before, scalars, *refs):
    core, expert = scalars[0], scalars[1]
    if with_weights:
        weights = refs[-2:]
        prepare(core, *refs[:2], *refs[-3:])
        refs = refs[2:-3]
    if before:
        lines = refs[0].shape[0]
        for i in range(before):
            refs[-1][i * lines : (i + 1) * lines, :] = refs[i][...]
        refs = (*refs[before:-1], refs[-1].at[before * lines :, :])
    hidden_ref, slope_ref, out_ref = refs[-3:]
    pieces, refs = taken(kinds, refs)
    if not with_weights:
        weights = refs[:2]
    lines, units = hidden_ref.shape
    wide, extras = units_of(core, pieces, rows, *weights)
    columns = []
    for extra in extras:
        column = gate_column(extra, expert, rows, experts)
        if len(kinds) > 1:
            column = picked(core, column[: rows // 2], column[rows // 2 :])
        columns.append(column)
    gate = stacked(columns)
    hidden = hidden_ref[...].astype(F32)
    out_ref[:, :units] = (gate * hidden).astype(BF16)
    out_ref[:, units : 2 * units] = (gate * slope_ref[...] * wide).astype(BF16)
    sums = jnp.sum(hidden * wide, axis=1, keepdims=True)
    lane = lax.broadcasted_iota(jnp.int32, (lines, LANES), 1)
    kept = jnp.zeros((lines, LANES), F32)
    for i, piece in enumerate(pieces_of(sums)):
        kept = jnp.where(lane == i, piece, kept)
    out_ref[:, 2 * units : 2 * units + LANES] = kept.astype(BF16)


def dots_rows(expert, dots, start, rows, width, experts):
    count = dots.shape[0]
    row = row_of(dots)
    if count < rows:
        blank = jnp.zeros((1, count), F32)
        row = jnp.concatenate([row, blank] if start == 0 else [blank, row], axis=1)
    out = jnp.zeros((EXTRA, width), F32)
    for piece, place in zip(pieces_of(row), table_parts(expert, rows, width, experts)):
        out = jnp.where(place, jnp.concatenate([piece] * (width // rows), axis=1), out)
    return out


def return_kernel(kind, at, first_row, count, experts, rows, scalars, mine_ref, arrived_ref, w_ref, *refs):
    core, expert = scalars[0], scalars[1]
    units, width = w_ref.shape
    lanes = slice(at, at + units + (LANES if at else 0))
    mine_all = mine_ref[first_row : first_row + count, lanes]
    arrived_all = arrived_ref[first_row : first_row + count, lanes]
    mine, arrived = mine_all[:, :units], arrived_all[:, :units]
    both = jnp.concatenate([picked(core, mine, arrived), picked(core, arrived, mine)], axis=0)
    part = dot_width(both, w_ref[...])
    with_dots = at > 0
    extra = [None, None]
    if with_dots:
        mine = jnp.sum(mine_all[:, units:].astype(F32), axis=1, keepdims=True)
        arrived = jnp.sum(arrived_all[:, units:].astype(F32), axis=1, keepdims=True)
        dots = [picked(core, mine, arrived), picked(core, arrived, mine)]
        starts = (0, count if count < rows else 0)
        extra = [
            dots_rows(expert, d, start, rows, width, experts) for d, start in zip(dots, starts)
        ]
    if kind == "far":
        for i, out_ref in enumerate(refs):
            out_ref[:count, :] = part[i * count : (i + 1) * count].astype(BF16)
            if with_dots:
                out_ref[count:, :] = extra[i].astype(BF16)
        return
    from_ahead, from_behind = refs[:2]
    if kind == "own":
        total = part + from_ahead[:rows, :].astype(F32) + from_behind[:rows, :].astype(F32)
        if not with_dots:
            refs[2][...] = total.astype(BF16)
            return
        routes_ref, out_ref, gates_ref = refs[2:]
        out_ref[...] = total.astype(BF16)
        table = extra[0] + extra[1]
        table = table + from_ahead[rows:, :].astype(F32) + from_behind[rows:, :].astype(F32)
        per_row = width // rows
        deep = -(-experts // per_row)
        routes = routes_ref[...]
        grads = jnp.zeros(routes.shape, F32)
        for e in range(experts):
            lanes = slice((e % per_row) * rows, (e % per_row + 1) * rows)
            line = e // per_row
            row = sum(table[i * deep + line : i * deep + line + 1, lanes] for i in range(3))
            grads = jnp.where(routes == e, row, grads)
        gates_ref[...] = grads
        return
    behind_ref, ahead_ref = refs[2:]
    behind, ahead = part[:count], part[count:]
    if kind == "join":
        half = count // 2
        behind_ref[:half, :] = (behind[:half] + from_ahead[:half, :].astype(F32)).astype(BF16)
        behind_ref[half:count, :] = behind[half:].astype(BF16)
        ahead_ref[:half, :] = ahead[:half].astype(BF16)
        ahead_ref[half:count, :] = (ahead[half:] + from_behind[:half, :].astype(F32)).astype(BF16)
    else:
        half = count
        behind_ref[:count, :] = (behind + from_ahead[:count, :].astype(F32)).astype(BF16)
        ahead_ref[:count, :] = (ahead + from_behind[:count, :].astype(F32)).astype(BF16)
    if with_dots:
        behind_ref[count:, :] = (extra[0] + from_ahead[half:, :].astype(F32)).astype(BF16)
        ahead_ref[count:, :] = (extra[1] + from_behind[half:, :].astype(F32)).astype(BF16)


def weight_kernel(blocks, rows, scalars, *refs):
    core = scalars[0]
    above, ends, own_other = refs[:3]
    own_ref, other_ref = refs[-2:]
    units, width = own_ref.shape[0] // 4, own_ref.shape[1]
    for i in range(2):
        lanes = slice(2 * i * units, 2 * (i + 1) * units)
        left = stacked([above[:, lanes], ends[:, lanes]])
        pieces = [("block", (ref,)) for ref in refs[3 + i * blocks : 3 + (i + 1) * blocks]]
        first_row = rows + EXTRA + (1 - i) * (rows // 2)
        pieces[-2] = (first_row, (pieces[-2][1][0], own_other))
        here, there, _ = zip(*(rows_of(core, p, rows, width) for p in pieces))
        for side, right in enumerate((here, there)):
            part = dot_rows(left, stacked(right))
            own = picked(core, part[:units], part[units:]).astype(BF16)
            other = picked(core, part[units:], part[:units]).astype(BF16)
            kept = jnp.where(scalars[2] == side, 1, 0)
            at = pl.ds(pl.multiple_of(kept * 2 * units + i * units, units), units)
            own_ref[at, :] = own
            other_ref[at, :] = other


def send_kernel(own_ref, came_ref, out_ref):
    out_ref[...] = (own_ref[...].astype(F32) + came_ref[...].astype(F32)).astype(BF16)


def add_kernel(own_ref, other_ref, came_ref, first_hbm, second_hbm, held_ref, sems):
    tiles, rows = held_ref.shape[0], held_ref.shape[1]
    copies = []
    for i in range(tiles):
        at = slice(i * rows, (i + 1) * rows)
        below = slice((tiles + i) * rows, (tiles + i + 1) * rows)
        kept = own_ref[below, :].astype(F32) + other_ref[below, :].astype(F32)
        held_ref[i] = kept + came_ref[at, :].astype(F32)
        out = first_hbm if i < tiles // 2 else second_hbm
        start = (i % (tiles // 2)) * rows
        copy = pltpu.make_async_copy(held_ref.at[i], out.at[pl.ds(start, rows), :], sems.at[i])
        copy.start()
        copies.append(copy)
    for copy in copies:
        copy.wait()


def per_device(tokens, routes, gates, w_in, w_out, cotangent):
    size = lax.axis_size("expert")
    n_dp = lax.axis_size("dp")
    rows, width = tokens.shape
    half = rows // 2
    experts = size * w_in.shape[0]
    core = lax.axis_index("tensor")
    place = lax.axis_index("expert")
    group = lax.axis_index("dp")
    order = ring_order(size)
    onward_pairs = [(order[i], order[(i + 1) % size]) for i in range(size)]
    back_pairs = [(b, a) for a, b in onward_pairs]
    steps = size // 2
    w_in, w_out = w_in[0], w_out[0]
    local_units = w_in.shape[0]
    units = 2 * local_units

    def both_ways(forth_value, back_value, name):
        with jax.named_scope("onward_" + name):
            forth = lax.ppermute(forth_value, "expert", onward_pairs)
        with jax.named_scope("back_" + name):
            return forth, lax.ppermute(back_value, "expert", back_pairs)

    first_core = lax.optimization_barrier(core == 0)
    core_now = jnp.where(first_core, 0, 1)
    scalars = jnp.stack([core_now, place, (core + group) % 2]).astype(jnp.int32)

    weight_shapes = [
        jax.ShapeDtypeStruct((units, width), BF16),
        jax.ShapeDtypeStruct((width, units), BF16),
        jax.ShapeDtypeStruct((width, units), BF16),
    ]

    def split(pieces):
        return tuple(p[0] for p in pieces), [v for p in pieces for v in p[1:]]

    def forward(pieces, weights):
        shape = (rows, units)
        raw = weights[0] is w_in
        kinds, operands = split(pieces)
        result = call(
            functools.partial(forward_kernel, kinds, rows, raw),
            [
                jax.ShapeDtypeStruct(shape, BF16),
                jax.ShapeDtypeStruct(shape, F32),
                *(weight_shapes if raw else ()),
            ],
            [*(weights if raw else ()), *operands, *(() if raw else weights[1:])],
            scalars,
            10**9,
        )
        return (result[:-3], result[-3:]) if raw else (result, weights)

    def backward(pieces, weights, hidden, slope, before=()):
        count = hidden.shape[0] * (1 + len(before))
        raw = weights[0] is w_out
        kinds, operands = split(pieces)
        result = call(
            functools.partial(backward_kernel, kinds, rows, experts, raw, len(before)),
            [
                jax.ShapeDtypeStruct((count, 2 * units + LANES), BF16),
                *(weight_shapes if raw else ()),
            ],
            [
                *(weights if raw else ()),
                *before,
                *operands,
                *(() if raw else weights[1:]),
                hidden,
                slope,
            ],
            scalars,
            10**9,
        )
        return (result[:-3], result[-3:]) if raw else (result, weights)

    def returned(kind, at, first_row, mine, arrived, weights, sums, more=()):
        count = rows if kind in ("join", "add") else half
        extra = EXTRA if at else 0
        if kind == "own":
            shapes = [jax.ShapeDtypeStruct((rows, width), BF16)]
            if at:
                shapes.append(jax.ShapeDtypeStruct(routes.shape[::-1], F32))
        else:
            shapes = [jax.ShapeDtypeStruct((count + extra, width), BF16)] * 2
        kernel = functools.partial(return_kernel, kind, at, first_row, count, experts, rows)
        operands = [mine, arrived, weights, *sums, *more]
        return call(kernel, shapes, operands, scalars, 30 * 10**8)

    apart_pairs = [(2 * i, 2 * j) for i, j in onward_pairs]
    apart_pairs += [(2 * i + 1, 2 * j + 1) for i, j in back_pairs]

    def apart(value, name):
        with jax.named_scope("onward_" + name):
            return lax.ppermute(value, ("expert", "tensor"), apart_pairs)

    payload = pl.pallas_call(
        functools.partial(payload_kernel, experts),
        out_shape=jax.ShapeDtypeStruct((rows + EXTRA, width), BF16),
        in_specs=[pl.BlockSpec(memory_space=pltpu.HBM)] * 3,
        out_specs=pl.BlockSpec(memory_space=pltpu.VMEM),
        scratch_shapes=[
            pltpu.VMEM(routes.shape[::-1], jnp.int32),
            pltpu.VMEM(gates.shape[::-1], F32),
            pltpu.SemaphoreType.DMA((4,)),
        ],
        compiler_params=pltpu.CompilerParams(vmem_limit_bytes=VMEM_LIMIT),
        cost_estimate=pl.CostEstimate(flops=10**9, bytes_accessed=0, transcendentals=0),
    )(routes.T, gates.T, cotangent)
    tokens_now = tied((tokens,), (scalars,))[0]
    ring = [both_ways(tokens_now, tokens_now, "tok1"), both_ways(payload, payload, "cot1")]

    in_all, out_all = (w_in, swap_cores(w_in, "weights")), ()

    tok_sent = call(
        first_tokens_kernel,
        [jax.ShapeDtypeStruct((rows, width), BF16)],
        [*ring[0]],
        scalars,
        2 * 10**9,
    )[0]
    tok_came = swap_cores(tok_sent, "tok1")
    def whole(pair, other):
        count = pair[0].shape[0]
        shape = [jax.ShapeDtypeStruct((count, 2 * width), BF16)]
        return call(whole_kernel, shape, [*pair, other], scalars, 10**6)[0]

    tok_whole = whole(ring[0], tok_came)
    seen = tied((*ring[1], w_out), (*in_all, tok_whole))
    cot_sent = pl.pallas_call(
        first_cotangent_kernel,
        out_shape=jax.ShapeDtypeStruct((2 * rows + EXTRA + units, width), BF16),
        in_specs=[pl.BlockSpec(memory_space=pltpu.SMEM)]
        + [pl.BlockSpec(memory_space=pltpu.VMEM)] * 4
        + [pl.BlockSpec(memory_space=pltpu.HBM)],
        out_specs=pl.BlockSpec(memory_space=pltpu.VMEM),
        scratch_shapes=[pltpu.SemaphoreType.DMA((2,))],
        compiler_params=pltpu.CompilerParams(vmem_limit_bytes=VMEM_LIMIT),
        cost_estimate=pl.CostEstimate(flops=10**9, bytes_accessed=0, transcendentals=0),
    )(scalars, *seen[:2], tokens, cotangent, seen[2])
    own_arrived = swap_cores(cot_sent, "cot1")
    out_all = (w_out, own_arrived)

    arrivals = [tok_whole, whole(ring[1], out_all[1])]
    outputs, lefts = [], []
    for turn in range(2 * steps):
        step = turn // 2 + 1
        name = ("tok", "cot")[turn % 2] + str(step + 1)
        now = arrivals[turn]
        if turn >= 2:
            now = arrivals[turn] = tied((now,), outputs[turn - 2])[0]
        if step < steps - 1:
            arrivals.append(apart(now, name))
        elif step == steps - 1:
            cut = half + (EXTRA if turn % 2 else 0)
            arrivals.append(apart(jnp.where(first_core, now[:cut], now[half:]), name))
        pieces = [("block", now)]
        if turn % 2 == 0:
            if step == steps:
                pieces = [(rows + EXTRA, tokens, own_arrived), *pieces]
            result, in_all = forward(pieces, in_all)
        else:
            if step == steps:
                pieces = [(rows + EXTRA + half, payload, own_arrived), *pieces]
            before = lefts if step == steps - 1 else ()
            result, out_all = backward(pieces, out_all, *outputs[-1], before)
            lefts.append(result[0])
        outputs.append(result)
    ends = lefts[steps - 1]
    lefts = lefts[steps - 2]
    lefts_arrived = swap_cores(tied((lefts,), (ends,))[0], "lefts")
    ends_arrived = swap_cores(ends, "ends")

    def weight_parts(after):
        operands = [lefts, tied((ends,), after)[0], own_arrived]
        for which in (1, 0):
            blocks = [arrivals[2 * step + which] for step in range(steps)]
            own = (tokens, payload)[which]
            operands += [*blocks[:-1], own, blocks[-1]]
        return pl.pallas_call(
            functools.partial(weight_kernel, steps + 1, rows),
            out_shape=[jax.ShapeDtypeStruct((2 * units, width), BF16)] * 2,
            in_specs=[pl.BlockSpec(memory_space=pltpu.SMEM)]
            + [pl.BlockSpec(memory_space=pltpu.VMEM)] * len(operands),
            out_specs=[pl.BlockSpec(memory_space=pltpu.VMEM)] * 2,
            compiler_params=pltpu.CompilerParams(vmem_limit_bytes=2 * VMEM_LIMIT),
            cost_estimate=pl.CostEstimate(flops=4 * 10**9, bytes_accessed=0, transcendentals=0),
        )(scalars, *operands)

    def over_groups(own, came):
        block = pl.BlockSpec((units // 4, width), lambda i: (i, 0))
        sent = pl.pallas_call(
            send_kernel,
            grid=(4,),
            out_shape=jax.ShapeDtypeStruct((units, width), BF16),
            in_specs=[block] * 2,
            out_specs=block,
            compiler_params=pltpu.CompilerParams(vmem_limit_bytes=VMEM_LIMIT),
            cost_estimate=pl.CostEstimate(flops=10**9, bytes_accessed=0, transcendentals=0),
        )(own, came)
        with jax.named_scope("groups"):
            return (sent,), lax.ppermute(sent, "dp", [(0, 1), (1, 0)])

    def over_many_groups(away, kept):
        mine = picked((core + group) % 2, kept, away)
        other = picked((core + group) % 2, away, kept)
        part = jnp.concatenate([picked(core, mine, other), picked(core, other, mine)], axis=1)
        across = part.shape[1] // n_dp
        slices = [
            lax.dynamic_slice_in_dim(part, ((group + shift) % n_dp) * across, across, axis=1)
            for shift in range(n_dp)
        ]
        total = slices[0]
        for shift in range(1, n_dp):
            pairs = [(i, (i + shift) % n_dp) for i in range(n_dp)]
            total = total + lax.ppermute(slices[shift].astype(BF16), "dp", pairs).astype(F32)
        return total[:local_units], total[local_units:]

    def summed(own, kept, came):
        tiles = 8
        return pl.pallas_call(
            add_kernel,
            out_shape=[jax.ShapeDtypeStruct((local_units, width), F32)] * 2,
            in_specs=[pl.BlockSpec(memory_space=pltpu.VMEM)] * 3,
            out_specs=[pl.BlockSpec(memory_space=pl.ANY)] * 2,
            scratch_shapes=[
                pltpu.VMEM((tiles, units // tiles, width), F32),
                pltpu.SemaphoreType.DMA((tiles,)),
            ],
            compiler_params=pltpu.CompilerParams(vmem_limit_bytes=VMEM_LIMIT),
            cost_estimate=pl.CostEstimate(flops=10**9, bytes_accessed=0, transcendentals=0),
        )(own, kept, came)

    def mixed_far(after):
        came = tied((ends_arrived,), after)[0]
        sent = returned("far", 0, half, ends, came, out_all[0], ())
        return sent, both_ways(sent[1], sent[0], "mixed")[::-1]

    def back_far(after):
        came = tied((ends_arrived,), after)[0]
        sent = returned("far", units, half, ends, came, in_all[0], ())
        return sent, both_ways(sent[1], sent[0], "grad")[::-1]

    def mixed_step(step, sums, after):
        kind = "join" if step == steps - 1 else "add"
        line = (step - 1) * rows
        sums = tied(sums, after)
        sent = returned(kind, 0, line, lefts, lefts_arrived, out_all[0], sums)
        return sent, both_ways(sent[1], sent[0], "mixed")[::-1]

    def back_step(step, sums, after):
        kind = "join" if step == steps - 1 else "add"
        line = (step - 1) * rows
        sums = tied(sums, after)
        sent = returned(kind, units, line, lefts, lefts_arrived, in_all[0], sums)
        return sent, both_ways(sent[1], sent[0], "grad")[::-1]

    parts, parts_other = weight_parts(())
    sent, mixed_in = mixed_far((parts, lefts_arrived))
    parts_came = swap_cores(tied((parts_other,), sent)[0], "parts")
    sent, back_in = back_far(sent)
    sent, mixed_in = mixed_step(steps - 1, mixed_in, sent)
    after = sent
    if n_dp == 2:
        parts_sent, came = over_groups(parts, tied((parts_came,), sent)[0])
        after = (*sent, *parts_sent)
    sent, back_in = back_step(steps - 1, back_in, after)
    for step in range(steps - 2, 0, -1):
        sent, mixed_in = mixed_step(step, mixed_in, sent)
        sent, back_in = back_step(step, back_in, sent)
    own = (0, ends, ends_arrived)
    mixed = returned("own", 0, *own, out_all[0], tied(mixed_in, sent))[0]
    if n_dp == 2:
        grad_out, grad_in = summed(parts, parts_came, tied((came,), (mixed,))[0])
    else:
        both = parts.astype(F32) + parts_came.astype(F32)
        grad_out, grad_in = over_many_groups(both[:units], both[units:])
    grad_tokens, grad_gates = returned(
        "own", units, *own, in_all[0], tied(back_in, (mixed, grad_out)), (routes.T,)
    )
    return (mixed, grad_tokens, grad_gates.T, grad_in[None], grad_out[None])


def solution(mesh):
    placed = (
        P(("dp", "expert"), "tensor"),
        P(("dp", "expert"), None),
        P(("dp", "expert"), None),
        P("expert", "tensor", None),
        P("expert", "tensor", None),
        P(("dp", "expert"), "tensor"),
    )
    return jax.shard_map(
        per_device,
        mesh=mesh,
        in_specs=placed,
        out_specs=(
            P(("dp", "expert"), "tensor"),
            P(("dp", "expert"), "tensor"),
            P(("dp", "expert"), None),
            P("expert", "tensor", "dp"),
            P("expert", "tensor", "dp"),
        ),
        check_vma=False,
    )
```
